512 devices in a mesh: grp: 2 (over x_hi), ctx: 32 (over z, x_lo), shd: 8 (over y, core).
Axes of the slice: x: 4 (x_hi: 2, x_lo: 2; x = x_hi * 2 + x_lo), y: 4, z: 16, core: 2. Of those that a mesh axis runs over, the one named last changes fastest.
Arguments:
- train_values: bfloat16 [2, 8192, 8192], P('grp', 'ctx', 'shd'), may hold values from -6 to 6
- train_gates: bfloat16 [2, 8192, 8192], P('grp', 'ctx', 'shd'), may hold values from -6 to 6
- train_writes: bfloat16 [2, 8192, 1024], P('grp', 'ctx', 'shd'), may hold values from -6 to 6
- train_reads: bfloat16 [2, 8192, 1024], P('grp', 'ctx', 'shd'), may hold values from -6 to 6
- train_steps: float32 [2, 8192, 128], P('grp', 'ctx', 'shd'), may hold values from -4 to 4
- out_cotangent: bfloat16 [2, 8192, 8192], P('grp', 'ctx', 'shd'), may hold values from -6 to 6
- head_params: float32 [3, 128], P(None, 'shd'), may hold values from -10.5 to 1.5, as said below
- norm_gain: float32 [8192], P('shd'), may hold values from 0.5 to 1.5
- slow_heads: float32 [3, 128], P(None, 'shd'), may hold values from -10.5 to 1.5, as said below
- slow_gain: float32 [8192], P('shd'), may hold values from 0.5 to 1.5
- roll_state: bfloat16 [128, 128, 64, 128], P(('grp', 'ctx'), 'shd'), may hold values from -6 to 6
- roll_values: bfloat16 [128, 4, 8192], P(('grp', 'ctx'), None, 'shd'), may hold values from -6 to 6
- roll_gates: bfloat16 [128, 4, 8192], P(('grp', 'ctx'), None, 'shd'), may hold values from -6 to 6
- roll_writes: bfloat16 [128, 4, 1024], P(('grp', 'ctx'), None, 'shd'), may hold values from -6 to 6
- roll_reads: bfloat16 [128, 4, 1024], P(('grp', 'ctx'), None, 'shd'), may hold values from -6 to 6
- roll_steps: float32 [128, 4, 128], P(('grp', 'ctx'), None, 'shd'), may hold values from -4 to 4
- roll_lengths: int32 [128], P(('grp', 'ctx')), may hold values from 1 to 4
Outputs:
- seq_out: bfloat16 [2, 8192, 8192], P('grp', 'ctx', 'shd')
- gradient_heads: float32 [3, 128], P(None, 'shd')
- gradient_gain: float32 [8192], P('shd')
- blend_heads: float32 [3, 128], P(None, 'shd')
- blend_gain: float32 [8192], P('shd')
- roll_out: bfloat16 [128, 4, 8192], P(('grp', 'ctx'), None, 'shd')
- roll_final: float32 [128, 128, 64, 128], P(('grp', 'ctx'), 'shd')
The draws below stay inside these ranges and needn't reach their ends.
Inputs may be any that keep to these rules, and one draw needn't show every extreme that they name: `head_params`: row 0 is the natural logarithm of each head's decay rate, row 1 the bias added to the raw step before softplus, row 2 the skip coefficient. `slow_heads`: rows as in head_params.
All inputs are finite; a program needn't handle non-finite values.
Results may differ from the reference program's by a relative error of at most 0.0017.
Values sent between devices are 32-bit elements; how exact they have to be, the bound alone decides.
No kernel may reach another device: no remote copies, remote signals or barrier semaphores. Data moves between devices by JAX's collectives and lax.ppermute only.
A program may use at most 128 MiB of HBM per device.

```python
import math
import jax
import jax.numpy as jnp
from jax import lax

HEADS = 128
HEAD_DIM = 64
STATE = 128
GROUPS = 8
INNER = 8192
BLOCK = 256
LENGTH = 8192
SEQS = 2
ROWS = 128
STEPS = 4


def head_law(key):
    slow_pick = jax.random.bernoulli(jax.random.fold_in(key, 1), 0.5, (HEADS,))
    slow_rates = jax.random.uniform(jax.random.fold_in(key, 2), (HEADS,), jnp.float32, math.log(3e-05), math.log(0.0003))
    fast_rates = jax.random.uniform(jax.random.fold_in(key, 3), (HEADS,), jnp.float32, math.log(0.003), math.log(0.05))
    rate_log = jnp.where(slow_pick, slow_rates, fast_rates)
    step_bias = jax.random.uniform(jax.random.fold_in(key, 4), (HEADS,), jnp.float32, -2.0, 1.0)
    skip_gain = jax.random.uniform(jax.random.fold_in(key, 5), (HEADS,), jnp.float32, 0.2, 1.5)
    return jnp.stack([rate_log, step_bias, skip_gain]).astype(jnp.float32)


def draw_head_params(key, part):
    return head_law(jax.random.fold_in(key, 5))


def draw_slow_heads(key, part):
    return head_law(jax.random.fold_in(key, 11))


def set_ends(drawn, rng, least, top_value):
    shape = drawn.shape
    index_at = [jax.random.randint(jax.random.fold_in(rng, axis), (), 0, shape[axis]) for axis in range(len(shape))]
    drawn = drawn.at[tuple(index_at)].set(least)
    longest = shape.index(max(shape))
    index_at[longest] = (index_at[longest] + 1) % shape[longest]
    return drawn.at[tuple(index_at)].set(top_value)


def steps_of(rng, dims, pieces, low, largest):
    factor_of, own = 1.0, jax.random.fold_in(rng, 6)
    for axis_at, blocks in pieces:
        heights = jnp.exp(jax.random.uniform(jax.random.fold_in(own, axis_at), (blocks,), jnp.float32, low / len(pieces), largest / len(pieces)))
        factor_of = factor_of * jnp.repeat(heights, dims[axis_at] // blocks).reshape([-1 if axis == axis_at else 1 for axis in range(len(dims))])
    return factor_of


def gaussian(key, dims, width, bound, split=(), kind=jnp.bfloat16):
    entries = width * jax.random.normal(key, dims, jnp.float32)
    if split:
        entries = entries * steps_of(key, dims, split, -0.22, 0.18)
    return jnp.clip(entries, -bound, bound).astype(kind)


def setup_inputs(seed: int = 0) -> dict:
    splits = jax.random.split(jax.random.key(seed), 18)
    return {
        "train_values": gaussian(splits[0], (SEQS, LENGTH, INNER), 1.0, 6.0, ((0, 2), (1, 32), (2, 8))),
        "train_gates": gaussian(splits[1], (SEQS, LENGTH, INNER), 1.0, 6.0, ((0, 2), (1, 32), (2, 8))),
        "train_writes": gaussian(splits[2], (SEQS, LENGTH, GROUPS * STATE), 1.0, 6.0, ((0, 2), (1, 32), (2, 8))),
        "train_reads": gaussian(splits[3], (SEQS, LENGTH, GROUPS * STATE), 1.0, 6.0, ((0, 2), (1, 32), (2, 8))),
        "train_steps": gaussian(splits[4], (SEQS, LENGTH, HEADS), 1.0, 4.0, ((0, 2), (1, 32), (2, 8)), jnp.float32),
        "out_cotangent": gaussian(splits[5], (SEQS, LENGTH, INNER), 1.0, 6.0, ((0, 2), (1, 32), (2, 8))),
        "head_params": draw_head_params(jax.random.fold_in(splits[17], 71), 0),
        "norm_gain": jnp.clip(1.0 + 0.1 * jax.random.normal(splits[7], (INNER,), jnp.float32), 0.5, 1.5),
        "slow_heads": draw_slow_heads(jax.random.fold_in(splits[17], 71), 0),
        "slow_gain": jnp.clip(1.0 + 0.1 * jax.random.normal(splits[9], (INNER,), jnp.float32), 0.5, 1.5),
        "roll_state": gaussian(splits[10], (ROWS, HEADS, HEAD_DIM, STATE), 1.0, 6.0, ((0, 64), (1, 8))),
        "roll_values": gaussian(splits[11], (ROWS, STEPS, INNER), 1.0, 6.0, ((0, 64), (2, 8))),
        "roll_gates": gaussian(splits[12], (ROWS, STEPS, INNER), 1.0, 6.0, ((0, 64), (2, 8))),
        "roll_writes": gaussian(splits[13], (ROWS, STEPS, GROUPS * STATE), 1.0, 6.0, ((0, 64), (2, 8))),
        "roll_reads": gaussian(splits[14], (ROWS, STEPS, GROUPS * STATE), 1.0, 6.0, ((0, 64), (2, 8))),
        "roll_steps": gaussian(splits[15], (ROWS, STEPS, HEADS), 1.0, 4.0, ((0, 64), (2, 8)), jnp.float32),
        "roll_lengths": set_ends(jax.random.randint(splits[16], (ROWS,), 1, STEPS + 1), jax.random.fold_in(splits[16], 1), 1, STEPS).astype(jnp.int32),
    }


HIGHEST = lax.Precision.HIGHEST
EPSILON = 1e-05
KEEP_SHARE = 0.75
STEP_RATE = 0.001

def block_terms(carried_in, block_data):
    state_now, offset = carried_in
    values, writes, reads, step_sizes, log_decay = block_data
    cumulative = jnp.cumsum(log_decay, axis=0)
    length = log_decay.shape[0]
    rows_iota = lax.broadcasted_iota(jnp.int32, (length, length), 0)
    cols_iota = lax.broadcasted_iota(jnp.int32, (length, length), 1)
    causal = (rows_iota >= cols_iota)[:, :, None]
    spread = jnp.where(causal, cumulative[:, None, :] - cumulative[None, :, :], 0.0)
    weights = jnp.where(causal, jnp.exp(spread), 0.0) * step_sizes[None, :, :]
    scores = jnp.einsum('thn,shn->tsh', reads, writes, precision=HIGHEST)
    inside = jnp.einsum('tsh,shp->thp', scores * weights, values, precision=HIGHEST)
    carried = jnp.exp(cumulative)[:, :, None] * jnp.einsum('thn,hpn->thp', reads, state_now, precision=HIGHEST)
    last_sum = cumulative[-1]
    tail_weight = jnp.exp(last_sum[None, :] - cumulative) * step_sizes
    fresh = jnp.einsum('sh,shp,shn->hpn', tail_weight, values, writes, precision=HIGHEST)
    new_state = jnp.exp(last_sum)[:, None, None] * state_now + fresh
    return ((new_state, offset + last_sum), (inside + carried, offset + cumulative))

def run_blocks(params, values, writes, reads, raw_steps, start_state):
    rate_log, step_bias, skip_gain = params
    step_sizes = jax.nn.softplus(raw_steps + step_bias)
    log_decay = -jnp.exp(rate_log) * step_sizes
    tokens, heads, head_width = values.shape
    block_count = tokens // BLOCK
    blocks = (values.reshape(block_count, BLOCK, heads, head_width), writes.reshape(block_count, BLOCK, heads, -1), reads.reshape(block_count, BLOCK, heads, -1), step_sizes.reshape(block_count, BLOCK, heads), log_decay.reshape(block_count, BLOCK, heads))
    offset = jnp.zeros((heads,), jnp.float32)
    (final, unused), (outputs, decay_sum) = lax.scan(jax.checkpoint(block_terms), (start_state, offset), blocks)
    local_out = outputs.reshape(tokens, heads, head_width) + skip_gain[:, None] * values
    return (local_out, final, decay_sum.reshape(tokens, heads))

def expand_groups(packed):
    grouped = packed.astype(jnp.float32).reshape(packed.shape[:-1] + (GROUPS, STATE))
    return jnp.repeat(grouped, HEADS // GROUPS, axis=-2)

def reference(train_values, train_gates, train_writes, train_reads, train_steps, out_cotangent, head_params, norm_gain, slow_heads, slow_gain, roll_state, roll_values, roll_gates, roll_writes, roll_reads, roll_steps, roll_lengths):
    params = (head_params[0], head_params[1], head_params[2])
    empty = jnp.zeros((HEADS, HEAD_DIM, STATE), jnp.float32)

    def train_loss(weights, gain):
        outputs = []
        loss_total = jnp.zeros((), jnp.float32)
        for seq_index in range(SEQS):
            values = train_values[seq_index].astype(jnp.float32).reshape(LENGTH, HEADS, HEAD_DIM)
            writes = expand_groups(train_writes[seq_index])
            reads = expand_groups(train_reads[seq_index])
            mixed_out, final, decay_sum = run_blocks(weights, values, writes, reads, train_steps[seq_index], empty)
            gated_out = mixed_out.reshape(LENGTH, INNER) * jax.nn.silu(train_gates[seq_index].astype(jnp.float32))
            inverse = lax.rsqrt(lax.optimization_barrier(jnp.mean(gated_out * gated_out, axis=1, keepdims=True)) + EPSILON)
            normed = gated_out * inverse * gain
            loss_total = loss_total + jnp.sum(normed * out_cotangent[seq_index].astype(jnp.float32))
            outputs.append(normed)
        return (loss_total, jnp.stack(outputs))
    loss_total, pullback, trained = jax.vjp(train_loss, params, norm_gain, has_aux=True)
    head_slope, gain_slope = pullback(jnp.ones_like(loss_total))
    gradient_heads = jnp.stack(list(head_slope))
    blend_heads = KEEP_SHARE * slow_heads + (1.0 - KEEP_SHARE) * (head_params - STEP_RATE * gradient_heads)
    blend_gain = KEEP_SHARE * slow_gain + (1.0 - KEEP_SHARE) * (norm_gain - STEP_RATE * gain_slope)
    decay_rate = jnp.exp(blend_heads[0])
    step_bias = blend_heads[1]
    skip_gain = blend_heads[2]

    def roll_row(row_items):
        start_state, row_values, row_gates, row_writes, row_reads, row_steps, row_length = row_items
        carried = start_state.astype(jnp.float32)
        outputs = []
        for turn_index in range(STEPS):
            active = row_length > turn_index
            step_sizes = jax.nn.softplus(row_steps[turn_index] + step_bias)
            decay_now = jnp.exp(-decay_rate * step_sizes)
            values = row_values[turn_index].astype(jnp.float32).reshape(HEADS, HEAD_DIM)
            writes = expand_groups(row_writes[turn_index])
            reads = expand_groups(row_reads[turn_index])
            update = decay_now[:, None, None] * carried + (step_sizes[:, None] * values)[:, :, None] * writes[:, None, :]
            carried = jnp.where(active, update, carried)
            read_out = jnp.einsum('hn,hpn->hp', reads, carried, precision=HIGHEST) + skip_gain[:, None] * values
            gated_out = read_out.reshape(INNER) * jax.nn.silu(row_gates[turn_index].astype(jnp.float32))
            inverse = lax.rsqrt(jnp.mean(gated_out * gated_out) + EPSILON)
            outputs.append(jnp.where(active, gated_out * inverse * blend_gain, 0.0))
        return (jnp.stack(outputs).astype(jnp.bfloat16), carried)
    roll_out, roll_final = lax.map(roll_row, (roll_state, roll_values, roll_gates, roll_writes, roll_reads, roll_steps, roll_lengths))
    return (trained.astype(jnp.bfloat16), gradient_heads, gain_slope, blend_heads, blend_gain, roll_out, roll_final)
```

```python
import jax
import jax.numpy as jnp
from jax import lax
from jax.experimental import pallas as pl
from jax.experimental.pallas import tpu as pltpu
from jax.sharding import Mesh
from jax.sharding import PartitionSpec as P

HEAD_DIM = 64
STATE = 128
INNER = 8192
STEPS = 4
CTX = ("ctx_0", "ctx_1")
GRP_CTX = ("grp", "ctx_0", "ctx_1")

F32 = jnp.float32
BF16 = jnp.bfloat16
HIGHEST = lax.Precision.HIGHEST
EPSILON = 1e-05
KEEP_SHARE = 0.75
STEP_RATE = 0.001

TOKENS = 256
HEADS = 16
UNITS = 1024
SLABS = 8
OWNERS = 32
ROWS = 32
NEVER = -1e30


def call(body, outs, *args, smem=(), vmem=None):
    specs = [
        pl.BlockSpec(memory_space=pltpu.SMEM if i in smem else pltpu.VMEM)
        for i in range(len(args))
    ]
    return pl.pallas_call(
        body,
        out_shape=[jax.ShapeDtypeStruct(shape, dtype) for shape, dtype in outs],
        in_specs=specs,
        out_specs=[pl.BlockSpec(memory_space=pltpu.VMEM) for _ in outs],
        compiler_params=pltpu.CompilerParams(vmem_limit_bytes=vmem or 40 * 2**20),
    )(*args)


def dot(a, b, over, precision=None):
    return lax.dot_general(
        a, b, (((over[0],), (over[1],)), ((), ())), precision=precision, preferred_element_type=F32
    )


def halves(a):
    top = a.astype(BF16)
    return top, (a - top.astype(F32)).astype(BF16)


def dot_left(a, b, over):
    top, rest = halves(a)
    return dot(top, b, over) + dot(rest, b, over)


def dot_right(a, b, over):
    top, rest = halves(b)
    return dot(a, top, over) + dot(a, rest, over)


def iota(shape, dim):
    return lax.broadcasted_iota(jnp.int32, shape, dim)


def first_head(rows):
    return iota((rows, 128), 1) < HEAD_DIM


def of_pair(table, slab):
    left = jnp.broadcast_to(table[:, 2 * slab : 2 * slab + 1], (table.shape[0], 128))
    right = jnp.broadcast_to(table[:, 2 * slab + 1 : 2 * slab + 2], (table.shape[0], 128))
    return jnp.where(first_head(table.shape[0]), left, right)


def head_mask(slab):
    return (iota((HEADS, 128), 0) == 2 * slab + iota((HEADS, 128), 1) // HEAD_DIM).astype(BF16)


def units(slab):
    return slice(128 * slab, 128 * slab + 128)


def silu(g):
    return g * (1.0 / (1.0 + jnp.exp(-g)))


def softplus(z):
    return jnp.maximum(z, 0.0) + jnp.log1p(jnp.exp(-jnp.abs(z)))


def sigmoid(z):
    return 1.0 / (1.0 + jnp.exp(-z))


def state_body(x, b, raw, heads, send, cum_out, turned):
    z = raw[...] + heads[1:2, :]
    step = softplus(z)
    slope = sigmoid(z)
    log_decay = -jnp.exp(heads[0:1, :]) * step
    lower = (iota((TOKENS, TOKENS), 0) >= iota((TOKENS, TOKENS), 1)).astype(F32)
    cum = dot(lower, log_decay, (1, 0), HIGHEST)
    cum_slope = dot(lower, slope, (1, 0), HIGHEST)
    cum_out[0] = cum
    cum_out[1] = cum_slope
    for i, table in enumerate((cum, cum_slope, step, slope)):
        turned[i] = table.T
    last = cum[TOKENS - 1 : TOKENS, :]
    tail = jnp.exp(last - cum) * step
    whole = jnp.exp(last)
    writes = b[...]
    for slab in range(SLABS):
        scaled = x[:, units(slab)].astype(F32) * of_pair(tail, slab)
        state = dot_left(scaled, writes, (0, 0))
        for q in range(4):
            owner = 4 * slab + q
            send[owner, 0:ROWS, :] = state[ROWS * q : ROWS * q + ROWS, :]
            send[owner, ROWS : ROWS + 8, :] = jnp.broadcast_to(
                whole[:, owner // 2 : owner // 2 + 1], (8, 128)
            )


def earlier_body(got, back):
    state = jnp.zeros((ROWS, STATE), F32)
    for k in range(OWNERS):
        back[k] = state
        state = got[k, ROWS : ROWS + 1, :] * state + got[k, 0:ROWS, :]


def later_body(decays, got, back):
    state = jnp.zeros((ROWS, STATE), F32)
    gains = jnp.zeros((8, STATE), F32)
    for k in reversed(range(OWNERS)):
        back[k, 0:ROWS, :] = state
        state = decays[k, ROWS : ROWS + 1, :] * state + got[k, 0:ROWS, :]
        gains = gains + got[k, ROWS : ROWS + 8, :]
    for k in range(OWNERS):
        back[k, ROWS : ROWS + 8, :] = gains


def causal():
    return iota((TOKENS, TOKENS), 0) >= iota((TOKENS, TOKENS), 1)


def inside_body(x, b, c, cum, turned, heads, out):
    scores = dot(c[...], b[...], (1, 1))
    mask = causal()
    left = first_head(TOKENS)
    for slab in range(SLABS):
        values = x[:, units(slab)]
        parts = []
        for h in (2 * slab, 2 * slab + 1):
            spread = cum[0, :, h : h + 1] - turned[0, h : h + 1, :]
            weights = jnp.exp(jnp.where(mask, spread, NEVER)) * turned[2, h : h + 1, :]
            parts.append(dot_left(scores * weights, values, (1, 0)))
        skip = of_pair(heads[2:3, :], slab)
        out[:, units(slab)] = jnp.where(left, parts[0], parts[1]) + skip * values.astype(F32)


def mixed_body(inside, state, c, cum, gates, cotangent, gain, carried, sums):
    reads = c[...]
    carry = jnp.exp(cum[0])
    squares = jnp.zeros((TOKENS, 128), F32)
    products = jnp.zeros((TOKENS, 128), F32)
    for slab in range(SLABS):
        part = dot_right(reads, state[units(slab), :], (1, 1)) * of_pair(carry, slab)
        carried[:, units(slab)] = part
        gated = (inside[:, units(slab)] + part) * silu(gates[:, units(slab)].astype(F32))
        squares = squares + gated * gated
        products = products + cotangent[:, units(slab)].astype(F32) * gain[:, units(slab)] * gated
    ones = jnp.ones((8, 128), F32)
    both = jnp.concatenate(
        [
            dot(ones, squares, (1, 1), HIGHEST)[0:4],
            dot(ones, products, (1, 1), HIGHEST)[0:4],
        ],
        axis=0,
    )
    for k in range(8):
        sums[k] = both


def slope_body(x, c, cum, gates, cotangent, gain, inside, carried, sums, seq_out, slopes, send):
    flat = sums[...].reshape(64, TOKENS)
    row = iota((64, 128), 0) % 8
    squares = dot(flat, (row == 0).astype(F32), (0, 0), HIGHEST)
    products = dot(flat, (row == 4).astype(F32), (0, 0), HIGHEST)
    inverse = lax.rsqrt(squares / INNER + EPSILON)
    pull = inverse * inverse * inverse * products / INNER
    carry = jnp.exp(cum[0])
    reads = c[...]
    for slab in range(SLABS):
        act = silu(gates[:, units(slab)].astype(F32))
        gated = (inside[:, units(slab)] + carried[:, units(slab)]) * act
        normed = gated * inverse
        weight = gain[:, units(slab)]
        cot = cotangent[:, units(slab)].astype(F32)
        seq_out[:, units(slab)] = (normed * weight).astype(BF16)
        gain_slope = jnp.sum(cot * normed, axis=0, keepdims=True)
        mixed_slope = (cot * weight * inverse - gated * pull) * act
        slopes[:, units(slab)] = mixed_slope
        state = dot_left(mixed_slope * of_pair(carry, slab), reads, (0, 0))
        for q in range(4):
            owner = 4 * slab + q
            send[owner, 0:ROWS, :] = state[ROWS * q : ROWS * q + ROWS, :]
            send[owner, ROWS : ROWS + 8, :] = jnp.broadcast_to(gain_slope, (8, 128))


def back_body(x, b, c, cum, turned, slopes, carried, out):
    scores = dot(c[...], b[...], (1, 1))
    mask = causal()
    left = first_head(TOKENS)
    carried_sum = jnp.zeros((HEADS, TOKENS), F32)
    skip_sum = jnp.zeros((HEADS, TOKENS), F32)
    for slab in range(SLABS):
        values = x[:, units(slab)]
        slope = slopes[:, units(slab)]
        member = head_mask(slab)
        carried_sum = carried_sum + dot_right(member, slope * carried[:, units(slab)], (1, 1))
        skip_sum = skip_sum + dot_right(member, slope * values.astype(F32), (1, 1))
        top, rest = halves(slope)
        for i in range(2):
            h = 2 * slab + i
            own = left if i == 0 else jnp.logical_not(left)
            value_h = jnp.where(own, values.astype(F32), 0.0).astype(BF16)
            product = dot(top, value_h, (1, 1)) + dot(rest, value_h, (1, 1))
            spread = cum[0, :, h : h + 1] - turned[0, h : h + 1, :]
            weights = jnp.exp(jnp.where(mask, spread, NEVER)) * turned[2, h : h + 1, :]
            each = product * scores * weights
            spread_slope = cum[1, :, h : h + 1] - turned[1, h : h + 1, :]
            out[0, h : h + 1, :] = jnp.sum(each, axis=0, keepdims=True)
            out[1, h : h + 1, :] = jnp.sum(each * spread, axis=0, keepdims=True)
            out[2, h : h + 1, :] = jnp.sum(each * spread_slope, axis=0, keepdims=True)
    out[3] = carried_sum
    out[4] = skip_sum


def heads_body(x, b, later, state, turned, inner, rate, send):
    writes = b[...]
    left_sum = jnp.zeros((HEADS, TOKENS), F32)
    lanes = []
    for slab in range(SLABS):
        pulled = later[4 * slab : 4 * slab + 4, 0:ROWS, :].reshape(128, STATE)
        met = dot_right(writes, pulled, (1, 1)) * x[:, units(slab)].astype(F32)
        left_sum = left_sum + dot_right(head_mask(slab), met, (1, 1))
        both = pulled * state[units(slab), :]
        lanes.append(jnp.sum(both[0:64], axis=0, keepdims=True))
        lanes.append(jnp.sum(both[64:128], axis=0, keepdims=True))
    through = jnp.sum(jnp.concatenate(lanes, axis=0), axis=1, keepdims=True)
    cum, cum_slope, step, slope = (turned[i] for i in range(4))
    last = cum[:, TOKENS - 1 : TOKENS]
    last_slope = cum_slope[:, TOKENS - 1 : TOKENS]
    fresh = left_sum * jnp.exp(last - cum) * step
    through = through * jnp.exp(last)

    def total(a):
        return jnp.sum(a, axis=1, keepdims=True)

    carried = inner[3]
    rate_slope = (
        total(inner[1] + carried * cum + fresh * (last - cum)) + last * through
    )
    bias_slope = total((inner[0] + fresh) * slope / step) - jnp.exp(rate[...]) * (
        total(inner[2] + carried * cum_slope + fresh * (last_slope - cum_slope))
        + last_slope * through
    )
    skip_slope = total(inner[4])
    lane = iota((HEADS, 8), 1)
    table = jnp.where(
        lane == 0, rate_slope, jnp.where(lane == 1, bias_slope, jnp.where(lane == 2, skip_slope, 0.0))
    )
    unit = (iota((HEADS, 128), 0) == iota((HEADS, 128), 1)).astype(F32)
    rows = dot(table, unit, (0, 0), HIGHEST)
    for k in range(4):
        send[k, 0:8, :] = rows
        for slab in range(SLABS):
            send[k, 8 + slab : 9 + slab, :] = later[4 * slab, ROWS : ROWS + 1, :]


def near_body(got, send, gains):
    rows = got[0, 0:8, :] + got[1, 0:8, :] + got[2, 0:8, :] + got[3, 0:8, :]
    for k in range(16):
        send[k] = rows
    gains[...] = got[0, 8:16, :] + got[2, 8:16, :]


def before_body(state, reads, writes, values, out):
    for r in range(2):
        out[r, 0:4, :] = dot(reads[r], state[r], (1, 1))
        meet = dot(writes[r], reads[r], (1, 1))
        out[r, 4:8, 0:128] = jnp.concatenate([meet, jnp.zeros((4, 124), F32)], axis=1)


def decode_body(
    lengths, got, heads, slow, raw, values, gates, writes, state, before, final, gated_out, sums,
    head_sum, blended,
):
    total = got[0]
    for k in range(1, 16):
        total = total + got[k]
    total = total[0:3, 0:HEADS]
    head_sum[...] = total
    blend = KEEP_SHARE * slow[...] + (1.0 - KEEP_SHARE) * (heads[...] - STEP_RATE * total)
    blended[...] = blend
    step = softplus(raw[...] + blend[1:2, :])
    log_decay = -jnp.exp(blend[0:1, :]) * step
    spread = (iota((HEADS, UNITS), 0) == iota((HEADS, UNITS), 1) // HEAD_DIM).astype(F32)
    table = jnp.concatenate([step, log_decay, jnp.broadcast_to(blend[2:3, :], (8, HEADS))], axis=0)
    wide = dot(table, spread, (1, 0), HIGHEST)
    skip = wide[16:17, :]
    row8 = iota((8, 128), 0)
    totals = jnp.zeros((8, 128), F32)
    for r in range(2):
        length = lengths[r]
        cum = []
        drive = []
        rows = values[r].astype(F32)
        for k in range(STEPS):
            at = 4 * r + k
            log_k = wide[8 + at : 9 + at, :]
            cum.append(log_k if k == 0 else cum[-1] + log_k)
            drive.append(wide[at : at + 1, :] * rows[k : k + 1, :])
        act = silu(gates[r].astype(F32))
        for k in range(STEPS):
            read = jnp.exp(cum[k]) * before[r, k : k + 1, :] + skip * rows[k : k + 1, :]
            for j in range(k + 1):
                kept = drive[j] if j == k else jnp.exp(cum[k] - cum[j]) * drive[j]
                read = read + kept * before[r, 4 + j : 5 + j, k : k + 1]
            gated = read * act[k : k + 1, :]
            gated_out[r, k : k + 1, :] = gated
            squares = jnp.sum(gated * gated, axis=1, keepdims=True)
            totals = jnp.where(row8 == 4 * r + k, squares, totals)
        end = cum[0]
        for k in range(1, STEPS):
            end = jnp.where(length > k, cum[k], end)
        weights = [jnp.exp(end)]
        for j in range(STEPS):
            live = length > j
            weights.append(jnp.where(live, jnp.exp(jnp.where(live, end - cum[j], 0.0)) * drive[j], 0.0))
        weights.append(jnp.zeros((3, UNITS), F32))
        weights = jnp.concatenate(weights, axis=0)
        wide_writes = jnp.concatenate(
            [jnp.zeros((1, STATE), F32), writes[r].astype(F32), jnp.zeros((3, STATE), F32)], axis=0
        )
        first = (iota((8, STATE), 0) == 0).astype(F32)
        kept = dot(weights, first, (0, 0), HIGHEST)
        fresh = dot(weights, wide_writes, (0, 0), HIGHEST)
        final[r] = kept * state[r].astype(F32) + fresh
    for k in range(8):
        sums[k] = totals


def rows_body(lengths, got, gated, gain, gain_slope, slow, out, gain_out):
    blend = KEEP_SHARE * slow[...] + (1.0 - KEEP_SHARE) * (gain[...] - STEP_RATE * gain_slope[...])
    gain_out[...] = blend
    total = got[0]
    for k in range(1, 8):
        total = total + got[k]
    inverse = lax.rsqrt(total / INNER + EPSILON)
    for slab in range(SLABS):
        for r in range(2):
            shown = gated[r, :, units(slab)] * inverse[4 * r : 4 * r + 4, :] * blend[slab : slab + 1, :]
            live = iota((STEPS, 128), 0) < lengths[r]
            out[r, :, units(slab)] = jnp.where(live, shown, 0.0).astype(BF16)


def exchange(value, axes):
    return lax.all_to_all(value, axes, split_axis=0, concat_axis=0, tiled=True)


def on_device(
    train_values,
    train_gates,
    train_writes,
    train_reads,
    train_steps,
    out_cotangent,
    head_params,
    norm_gain,
    slow_heads,
    slow_gain,
    roll_state,
    roll_values,
    roll_gates,
    roll_writes,
    roll_reads,
    roll_steps,
    roll_lengths,
):
    x, gates, cotangent = train_values[0], train_gates[0], out_cotangent[0]
    b, c, raw = train_writes[0], train_reads[0], train_steps[0]
    gain = norm_gain.reshape(1, UNITS)
    wide = (TOKENS, UNITS)
    piece = (OWNERS, ROWS + 8, STATE)

    send, cum, turned = call(
        state_body,
        [(piece, F32), ((2, TOKENS, HEADS), F32), ((4, HEADS, TOKENS), F32)],
        x, b, raw, head_params,
    )
    got = exchange(send, CTX)
    (inside,) = call(inside_body, [(wide, F32)], x, b, c, cum, turned, head_params)
    (back,) = call(earlier_body, [((OWNERS, ROWS, STATE), F32)], got)
    state_in = exchange(back, CTX).reshape(UNITS, STATE)
    carried, sums = call(
        mixed_body,
        [(wide, F32), ((8, 8, TOKENS), F32)],
        inside, state_in, c, cum, gates, cotangent, gain,
    )
    sums = exchange(sums, "shd")
    seq_out, slopes, send = call(
        slope_body,
        [(wide, BF16), (wide, F32), (piece, F32)],
        x, c, cum, gates, cotangent, gain, inside, carried, sums,
    )
    upward = exchange(send, CTX)
    (inner,) = call(
        back_body, [((5, HEADS, TOKENS), F32)], x, b, c, cum, turned, slopes, carried
    )
    flat_state = roll_state.reshape(2, UNITS, STATE)
    (before,) = call(
        before_body, [((2, 8, UNITS), F32)], flat_state, roll_reads, roll_writes, roll_values
    )
    (back,) = call(later_body, [(piece, F32)], got, upward)
    later = exchange(back, CTX)
    (send,) = call(
        heads_body,
        [((4, 16, 128), F32)],
        x, b, later, state_in, turned, inner, head_params[0].reshape(HEADS, 1),
    )
    near = exchange(send, ("grp", "ctx_1"))
    send, gain_slope = call(near_body, [((16, 8, 128), F32), ((8, 128), F32)], near)
    far = exchange(send, "ctx_0")
    final, gated, sums, head_sum, blend_heads = call(
        decode_body,
        [
            ((2, UNITS, STATE), F32),
            ((2, STEPS, UNITS), F32),
            ((8, 8, 128), F32),
            ((3, HEADS), F32),
            ((3, HEADS), F32),
        ],
        roll_lengths, far, head_params, slow_heads, roll_steps.reshape(8, HEADS), roll_values,
        roll_gates, roll_writes, flat_state, before,
        smem=(0,),
    )
    sums = exchange(sums, "shd")
    roll_out, blend_gain = call(
        rows_body,
        [((2, STEPS, UNITS), BF16), ((8, 128), F32)],
        roll_lengths, sums, gated, norm_gain.reshape(8, 128), gain_slope, slow_gain.reshape(8, 128),
        smem=(0,),
    )
    return (
        seq_out[None],
        head_sum,
        gain_slope.reshape(UNITS),
        blend_heads,
        blend_gain.reshape(UNITS),
        roll_out,
        final.reshape(2, HEADS, HEAD_DIM, STATE),
    )


def solution(mesh):
    split = Mesh(
        mesh.devices.reshape(mesh.shape["grp"], 16, 2, mesh.shape["shd"]),
        ("grp", "ctx_0", "ctx_1", "shd"),
    )
    return jax.shard_map(
        on_device,
        mesh=split,
        in_specs=(
            P("grp", CTX, "shd"),
            P("grp", CTX, "shd"),
            P("grp", CTX, "shd"),
            P("grp", CTX, "shd"),
            P("grp", CTX, "shd"),
            P("grp", CTX, "shd"),
            P(None, "shd"),
            P("shd"),
            P(None, "shd"),
            P("shd"),
            P(GRP_CTX, "shd", None, None),
            P(GRP_CTX, None, "shd"),
            P(GRP_CTX, None, "shd"),
            P(GRP_CTX, None, "shd"),
            P(GRP_CTX, None, "shd"),
            P(GRP_CTX, None, "shd"),
            P(GRP_CTX),
        ),
        out_specs=(
            P("grp", CTX, "shd"),
            P(None, "shd"),
            P("shd"),
            P(None, "shd"),
            P("shd"),
            P(GRP_CTX, None, "shd"),
            P(GRP_CTX, "shd", None, None),
        ),
        check_vma=False,
    )
```

```python
import jax
import jax.numpy as jnp
from jax import lax
from jax.experimental import pallas as pl
from jax.experimental.pallas import tpu as pltpu
from jax.sharding import Mesh
from jax.sharding import PartitionSpec as P

HEAD_DIM = 64
STATE = 128
INNER = 8192
STEPS = 4
CTX = ("far", "near", "ctx_1")
GRP_CTX = ("grp", "far", "near", "ctx_1")
GROUP = ("near", "ctx_1")

F32 = jnp.float32
BF16 = jnp.bfloat16
HIGHEST = lax.Precision.HIGHEST
EPSILON = 1e-05
KEEP_SHARE = 0.75
STEP_RATE = 0.001

TOKENS = 256
HEADS = 16
UNITS = 1024
SLABS = 8
MEMBERS = 8
FAR = 4
NEVER = -1e30


def call(body, outs, *args, smem=(), vmem=None):
    specs = [
        pl.BlockSpec(memory_space=pltpu.SMEM if i in smem else pltpu.VMEM)
        for i in range(len(args))
    ]
    return pl.pallas_call(
        body,
        out_shape=[jax.ShapeDtypeStruct(shape, dtype) for shape, dtype in outs],
        in_specs=specs,
        out_specs=[pl.BlockSpec(memory_space=pltpu.VMEM) for _ in outs],
        compiler_params=pltpu.CompilerParams(vmem_limit_bytes=vmem or 40 * 2**20),
    )(*args)


def dot(a, b, over, precision=None):
    return lax.dot_general(
        a, b, (((over[0],), (over[1],)), ((), ())), precision=precision, preferred_element_type=F32
    )


def halves(a):
    top = a.astype(BF16)
    return top, (a - top.astype(F32)).astype(BF16)


def dot_left(a, b, over):
    top, rest = halves(a)
    return dot(top, b, over) + dot(rest, b, over)


def dot_right(a, b, over):
    top, rest = halves(b)
    return dot(a, top, over) + dot(a, rest, over)


def iota(shape, dim):
    return lax.broadcasted_iota(jnp.int32, shape, dim)


def first_head(rows):
    return iota((rows, 128), 1) < HEAD_DIM


def of_pair(table, slab):
    left = jnp.broadcast_to(table[:, 2 * slab : 2 * slab + 1], (table.shape[0], 128))
    right = jnp.broadcast_to(table[:, 2 * slab + 1 : 2 * slab + 2], (table.shape[0], 128))
    return jnp.where(first_head(table.shape[0]), left, right)


def head_mask(slab):
    return (iota((HEADS, 128), 0) == 2 * slab + iota((HEADS, 128), 1) // HEAD_DIM).astype(BF16)


def units(slab):
    return slice(128 * slab, 128 * slab + 128)


def silu(g):
    return g * (1.0 / (1.0 + jnp.exp(-g)))


def softplus(z):
    return jnp.maximum(z, 0.0) + jnp.log1p(jnp.exp(-jnp.abs(z)))


def sigmoid(z):
    return 1.0 / (1.0 + jnp.exp(-z))


def column(heads, row):
    same = iota((HEADS, HEADS), 0) == iota((HEADS, HEADS), 1)
    return jnp.sum(jnp.where(same, heads[row : row + 1, :], 0.0), axis=1, keepdims=True)


def state_body(x, b, raw, heads, send, cum_out, turned):
    z = raw[...] + column(heads, 1)
    step = softplus(z)
    slope = sigmoid(z)
    log_decay = -jnp.exp(column(heads, 0)) * step
    upper = (iota((TOKENS, TOKENS), 0) <= iota((TOKENS, TOKENS), 1)).astype(F32)
    both = dot(jnp.concatenate([log_decay, slope], axis=0), upper, (1, 0), HIGHEST)
    cum = both[0:HEADS]
    last = cum[:, TOKENS - 1 : TOKENS]
    tail = (jnp.exp(last - cum) * step).T
    whole = jnp.exp(last)
    turned[0] = cum
    turned[1] = both[HEADS:]
    turned[2] = step
    turned[3] = slope
    cum_out[0] = cum.T
    cum_out[1] = both[HEADS:].T
    writes = b[...]
    for slab in range(SLABS):
        scaled = x[:, units(slab)].astype(F32) * of_pair(tail, slab)
        send[slab, 0:128, :] = dot_left(scaled, writes, (0, 0))
        for i in range(2):
            h = 2 * slab + i
            send[slab, 128 + 4 * i : 132 + 4 * i, :] = jnp.broadcast_to(whole[h : h + 1, :], (4, 128))


def of_rows(pair):
    return jnp.concatenate(
        [jnp.broadcast_to(pair[0:1, :], (64, 128)), jnp.broadcast_to(pair[4:5, :], (64, 128))], axis=0
    )


def group_body(got, decays, total):
    state = got[0, 0:128, :]
    whole = got[0, 128:136, :]
    decays[0] = whole
    for k in range(1, MEMBERS):
        pair = got[k, 128:136, :]
        decays[k] = pair
        state = of_rows(pair) * state + got[k, 0:128, :]
        whole = pair * whole
    total[0:128, :] = state
    total[128:136, :] = whole


def from_groups(three, two, one):
    state = three[0:128, :]
    for group in (two, one):
        state = of_rows(group[128:136, :]) * state + group[0:128, :]
    return state


def earlier_body(got, three, two, one, back):
    state = from_groups(three, two, one)
    for k in range(MEMBERS):
        back[k] = state
        if k < MEMBERS - 1:
            state = of_rows(got[k, 128:136, :]) * state + got[k, 0:128, :]


def later_group_body(decays, got, total):
    state = got[MEMBERS - 1]
    whole = decays[MEMBERS - 1]
    for k in reversed(range(MEMBERS - 1)):
        state = of_rows(decays[k]) * state + got[k]
        whole = decays[k] * whole
    total[0:128, :] = state
    total[128:136, :] = whole


def later_body(decays, got, three, two, one, back):
    state = from_groups(three, two, one)
    for k in reversed(range(MEMBERS)):
        back[k] = state
        if k:
            state = of_rows(decays[k]) * state + got[k]


def causal():
    return iota((TOKENS, TOKENS), 0) >= iota((TOKENS, TOKENS), 1)


def inside_body(x, b, c, cum, turned, heads, out):
    scores = dot(c[...], b[...], (1, 1))
    mask = causal()
    left = first_head(TOKENS)
    for slab in range(SLABS):
        values = x[:, units(slab)]
        parts = []
        for h in (2 * slab, 2 * slab + 1):
            spread = cum[0, :, h : h + 1] - turned[0, h : h + 1, :]
            weights = jnp.exp(jnp.where(mask, spread, NEVER)) * turned[2, h : h + 1, :]
            parts.append(dot_left(scores * weights, values, (1, 0)))
        skip = of_pair(heads[2:3, :], slab)
        out[:, units(slab)] = jnp.where(left, parts[0], parts[1]) + skip * values.astype(F32)


def mixed_body(inside, state, c, cum, gates, cotangent, gain, carried, sums):
    reads = c[...]
    carry = jnp.exp(cum[0])
    squares = jnp.zeros((TOKENS, 128), F32)
    products = jnp.zeros((TOKENS, 128), F32)
    for slab in range(SLABS):
        part = dot_right(reads, state[units(slab), :], (1, 1)) * of_pair(carry, slab)
        carried[:, units(slab)] = part
        gated = (inside[:, units(slab)] + part) * silu(gates[:, units(slab)].astype(F32))
        squares = squares + gated * gated
        products = products + cotangent[:, units(slab)].astype(F32) * gain[:, units(slab)] * gated
    ones = jnp.ones((8, 128), F32)
    squares = dot(ones, squares, (1, 1), HIGHEST)
    products = dot(ones, products, (1, 1), HIGHEST)
    both = jnp.concatenate(
        [
            squares[0:1, 0:128],
            squares[0:1, 128:256],
            products[0:1, 0:128],
            products[0:1, 128:256],
            jnp.zeros((4, 128), F32),
        ],
        axis=0,
    )
    for k in range(8):
        sums[k] = both


def spread_sum(flat, first):
    row = iota((64, 128), 0) % 8
    return jnp.concatenate(
        [dot(flat, (row == first + i).astype(F32), (0, 0), HIGHEST) for i in range(2)], axis=0
    )


def slope_body(x, c, cum, gates, cotangent, gain, inside, carried, sums, seq_out, slopes, send, gains):
    flat = sums[...].reshape(64, 128)
    squares = spread_sum(flat, 0)
    products = spread_sum(flat, 2)
    inverse = lax.rsqrt(squares / INNER + EPSILON)
    pull = inverse * inverse * inverse * products / INNER
    carry = jnp.exp(cum[0])
    reads = c[...]
    for slab in range(SLABS):
        act = silu(gates[:, units(slab)].astype(F32))
        gated = (inside[:, units(slab)] + carried[:, units(slab)]) * act
        normed = gated * inverse
        weight = gain[:, units(slab)]
        cot = cotangent[:, units(slab)].astype(F32)
        seq_out[:, units(slab)] = (normed * weight).astype(BF16)
        gain_slope = jnp.sum(cot * normed, axis=0, keepdims=True)
        mixed_slope = (cot * weight * inverse - gated * pull) * act
        slopes[:, units(slab)] = mixed_slope
        send[slab] = dot_left(mixed_slope * of_pair(carry, slab), reads, (0, 0))
        gains[slab : slab + 1, :] = gain_slope


def back_body(x, b, c, cum, turned, slopes, carried, out):
    scores = dot(c[...], b[...], (1, 1))
    mask = causal()
    left = first_head(TOKENS)
    carried_sum = jnp.zeros((HEADS, TOKENS), F32)
    skip_sum = jnp.zeros((HEADS, TOKENS), F32)
    for slab in range(SLABS):
        values = x[:, units(slab)]
        slope = slopes[:, units(slab)]
        member = head_mask(slab)
        carried_sum = carried_sum + dot_right(member, slope * carried[:, units(slab)], (1, 1))
        skip_sum = skip_sum + dot_right(member, slope * values.astype(F32), (1, 1))
        top, rest = halves(slope)
        for i in range(2):
            h = 2 * slab + i
            own = left if i == 0 else jnp.logical_not(left)
            value_h = jnp.where(own, values.astype(F32), 0.0).astype(BF16)
            product = dot(top, value_h, (1, 1)) + dot(rest, value_h, (1, 1))
            spread = cum[0, :, h : h + 1] - turned[0, h : h + 1, :]
            weights = jnp.exp(jnp.where(mask, spread, NEVER)) * turned[2, h : h + 1, :]
            each = product * scores * weights
            spread_slope = cum[1, :, h : h + 1] - turned[1, h : h + 1, :]
            out[0, h : h + 1, :] = jnp.sum(each, axis=0, keepdims=True)
            out[1, h : h + 1, :] = jnp.sum(each * spread, axis=0, keepdims=True)
            out[2, h : h + 1, :] = jnp.sum(each * spread_slope, axis=0, keepdims=True)
    out[3] = carried_sum
    out[4] = skip_sum


def heads_body(x, b, later, state, turned, inner, heads, gains, send):
    writes = b[...]
    left_sum = jnp.zeros((HEADS, TOKENS), F32)
    lanes = []
    for slab in range(SLABS):
        pulled = later[slab]
        met = dot_right(writes, pulled, (1, 1)) * x[:, units(slab)].astype(F32)
        left_sum = left_sum + dot_right(head_mask(slab), met, (1, 1))
        both = pulled * state[units(slab), :]
        lanes.append(jnp.sum(both[0:64], axis=0, keepdims=True))
        lanes.append(jnp.sum(both[64:128], axis=0, keepdims=True))
    through = jnp.sum(jnp.concatenate(lanes, axis=0), axis=1, keepdims=True)
    cum, cum_slope, step, slope = (turned[i] for i in range(4))
    last = cum[:, TOKENS - 1 : TOKENS]
    last_slope = cum_slope[:, TOKENS - 1 : TOKENS]
    fresh = left_sum * jnp.exp(last - cum) * step
    through = through * jnp.exp(last)

    def total(a):
        return jnp.sum(a, axis=1, keepdims=True)

    carried = inner[3]
    rate_slope = (
        total(inner[1] + carried * cum + fresh * (last - cum)) + last * through
    )
    bias_slope = total((inner[0] + fresh) * slope / step) - jnp.exp(column(heads, 0)) * (
        total(inner[2] + carried * cum_slope + fresh * (last_slope - cum_slope))
        + last_slope * through
    )
    skip_slope = total(inner[4])
    lane = iota((HEADS, 8), 1)
    table = jnp.where(
        lane == 0, rate_slope, jnp.where(lane == 1, bias_slope, jnp.where(lane == 2, skip_slope, 0.0))
    )
    unit = (iota((HEADS, 128), 0) == iota((HEADS, 128), 1)).astype(F32)
    rows = dot(table, unit, (0, 0), HIGHEST)
    for k in range(4):
        send[k, 0:8, :] = rows
        send[k, 8:16, :] = gains[...]


def near_body(got, send):
    rows = got[0] + got[1] + got[2] + got[3]
    for k in range(16):
        send[k] = rows


def before_body(state, reads, writes, out):
    for r in range(2):
        out[r, 0:4, :] = dot(reads[r], state[r], (1, 1))
        meet = dot(writes[r], reads[r], (1, 1))
        out[r, 4:8, 0:128] = jnp.concatenate([meet, jnp.zeros((4, 124), F32)], axis=1)


def decode_body(
    lengths, got, heads, slow, raw, values, gates, before, gated_out, sums, weights_out, gains,
    head_sum, blended,
):
    total = got[0]
    for k in range(1, 16):
        total = total + got[k]
    gains[...] = total[8:16, :]
    total = total[0:3, 0:HEADS]
    head_sum[...] = total
    blend = KEEP_SHARE * slow[...] + (1.0 - KEEP_SHARE) * (heads[...] - STEP_RATE * total)
    blended[...] = blend
    step = softplus(raw[...] + blend[1:2, :])
    log_decay = -jnp.exp(blend[0:1, :]) * step
    spread = (iota((HEADS, UNITS), 0) == iota((HEADS, UNITS), 1) // HEAD_DIM).astype(F32)
    table = jnp.concatenate([step, log_decay, jnp.broadcast_to(blend[2:3, :], (8, HEADS))], axis=0)
    wide = dot(table, spread, (1, 0), HIGHEST)
    skip = wide[16:17, :]
    row8 = iota((8, 128), 0)
    totals = jnp.zeros((8, 128), F32)
    for r in range(2):
        length = lengths[r]
        cum = []
        drive = []
        rows = values[r].astype(F32)
        for k in range(STEPS):
            at = 4 * r + k
            log_k = wide[8 + at : 9 + at, :]
            cum.append(log_k if k == 0 else cum[-1] + log_k)
            drive.append(wide[at : at + 1, :] * rows[k : k + 1, :])
        act = silu(gates[r].astype(F32))
        for k in range(STEPS):
            read = jnp.exp(cum[k]) * before[r, k : k + 1, :] + skip * rows[k : k + 1, :]
            for j in range(k + 1):
                kept = drive[j] if j == k else jnp.exp(cum[k] - cum[j]) * drive[j]
                read = read + kept * before[r, 4 + j : 5 + j, k : k + 1]
            gated = read * act[k : k + 1, :]
            gated_out[r, k : k + 1, :] = gated
            squares = jnp.sum(gated * gated, axis=1, keepdims=True)
            totals = jnp.where(row8 == 4 * r + k, squares, totals)
        end = cum[0]
        for k in range(1, STEPS):
            end = jnp.where(length > k, cum[k], end)
        weights = [jnp.exp(end)]
        for j in range(STEPS):
            live = length > j
            weights.append(jnp.where(live, jnp.exp(jnp.where(live, end - cum[j], 0.0)) * drive[j], 0.0))
        weights.append(jnp.zeros((3, UNITS), F32))
        weights_out[r] = jnp.concatenate(weights, axis=0)
    for k in range(8):
        sums[k] = totals


def final_body(weights, writes, state, final):
    first = (iota((8, STATE), 0) == 0).astype(F32)
    for r in range(2):
        wide_writes = jnp.concatenate(
            [jnp.zeros((1, STATE), F32), writes[r].astype(F32), jnp.zeros((3, STATE), F32)], axis=0
        )
        kept = dot(weights[r], first, (0, 0), HIGHEST)
        fresh = dot(weights[r], wide_writes, (0, 0), HIGHEST)
        final[r] = kept * state[r].astype(F32) + fresh


def rows_body(lengths, got, gated, gain, gain_slope, slow, out, gain_out):
    blend = KEEP_SHARE * slow[...] + (1.0 - KEEP_SHARE) * (gain[...] - STEP_RATE * gain_slope[...])
    gain_out[...] = blend
    total = got[0]
    for k in range(1, 8):
        total = total + got[k]
    inverse = lax.rsqrt(total / INNER + EPSILON)
    for slab in range(SLABS):
        for r in range(2):
            shown = gated[r, :, units(slab)] * inverse[4 * r : 4 * r + 4, :] * blend[slab : slab + 1, :]
            live = iota((STEPS, 128), 0) < lengths[r]
            out[r, :, units(slab)] = jnp.where(live, shown, 0.0).astype(BF16)


def exchange(value, axes):
    return lax.all_to_all(value, axes, split_axis=0, concat_axis=0, tiled=True)


def shifted(value, by):
    pairs = [(k, k + by) for k in range(FAR) if 0 <= k + by < FAR]
    return lax.ppermute(value, "far", pairs)


def on_device(
    train_values,
    train_gates,
    train_writes,
    train_reads,
    train_steps,
    out_cotangent,
    head_params,
    norm_gain,
    slow_heads,
    slow_gain,
    roll_state,
    roll_values,
    roll_gates,
    roll_writes,
    roll_reads,
    roll_steps,
    roll_lengths,
):
    x, gates, cotangent = train_values[0], train_gates[0], out_cotangent[0]
    b, c, raw = train_writes[0], train_reads[0], train_steps[0].T
    gain = norm_gain.reshape(1, UNITS)
    wide = (TOKENS, UNITS)
    group = (136, STATE)
    tile = (8, 8, 128)

    send, cum, turned = call(
        state_body,
        [((MEMBERS, 136, STATE), F32), ((2, TOKENS, HEADS), F32), ((4, HEADS, TOKENS), F32)],
        x, b, raw, head_params,
    )
    got = exchange(send, GROUP)
    decays, total = call(group_body, [(tile, F32), (group, F32)], got)
    groups = [shifted(total, by) for by in (3, 2, 1)]
    (inside,) = call(inside_body, [(wide, F32)], x, b, c, cum, turned, head_params)
    (back,) = call(earlier_body, [((MEMBERS, 128, STATE), F32)], got, *groups)
    state_in = exchange(back, GROUP).reshape(UNITS, STATE)
    carried, sums = call(
        mixed_body, [(wide, F32), (tile, F32)], inside, state_in, c, cum, gates, cotangent, gain
    )
    sums = exchange(sums, "shd")
    seq_out, slopes, send, gains = call(
        slope_body,
        [(wide, BF16), (wide, F32), ((MEMBERS, 128, STATE), F32), ((8, 128), F32)],
        x, c, cum, gates, cotangent, gain, inside, carried, sums,
    )
    upward = exchange(send, GROUP)
    (total,) = call(later_group_body, [(group, F32)], decays, upward)
    groups = [shifted(total, -by) for by in (3, 2, 1)]
    (inner,) = call(
        back_body, [((5, HEADS, TOKENS), F32)], x, b, c, cum, turned, slopes, carried
    )
    flat_state = roll_state.reshape(2, UNITS, STATE)
    (before,) = call(before_body, [((2, 8, UNITS), F32)], flat_state, roll_reads, roll_writes)
    (back,) = call(later_body, [((MEMBERS, 128, STATE), F32)], decays, upward, *groups)
    later = exchange(back, GROUP)
    (send,) = call(
        heads_body,
        [((4, 16, 128), F32)],
        x, b, later, state_in, turned, inner, head_params, gains,
    )
    near = exchange(send, ("grp", "ctx_1"))
    (send,) = call(near_body, [((16, 16, 128), F32)], near)
    far = exchange(send, ("far", "near"))
    gated, sums, weights, gain_slope, head_sum, blend_heads = call(
        decode_body,
        [
            ((2, STEPS, UNITS), F32),
            (tile, F32),
            ((2, 8, UNITS), F32),
            ((8, 128), F32),
            ((3, HEADS), F32),
            ((3, HEADS), F32),
        ],
        roll_lengths, far, head_params, slow_heads, roll_steps.reshape(8, HEADS), roll_values,
        roll_gates, before,
        smem=(0,),
    )
    sums = exchange(sums, "shd")
    (final,) = call(
        final_body, [((2, UNITS, STATE), F32)], weights, roll_writes, flat_state
    )
    roll_out, blend_gain = call(
        rows_body,
        [((2, STEPS, UNITS), BF16), ((8, 128), F32)],
        roll_lengths, sums, gated, norm_gain.reshape(8, 128), gain_slope, slow_gain.reshape(8, 128),
        smem=(0,),
    )
    return (
        seq_out[None],
        head_sum,
        gain_slope.reshape(UNITS),
        blend_heads,
        blend_gain.reshape(UNITS),
        roll_out,
        final.reshape(2, HEADS, HEAD_DIM, STATE),
    )


def solution(mesh):
    split = Mesh(
        mesh.devices.reshape(mesh.shape["grp"], FAR, 4, 2, mesh.shape["shd"]),
        ("grp", "far", "near", "ctx_1", "shd"),
    )
    return jax.shard_map(
        on_device,
        mesh=split,
        in_specs=(
            P("grp", CTX, "shd"),
            P("grp", CTX, "shd"),
            P("grp", CTX, "shd"),
            P("grp", CTX, "shd"),
            P("grp", CTX, "shd"),
            P("grp", CTX, "shd"),
            P(None, "shd"),
            P("shd"),
            P(None, "shd"),
            P("shd"),
            P(GRP_CTX, "shd", None, None),
            P(GRP_CTX, None, "shd"),
            P(GRP_CTX, None, "shd"),
            P(GRP_CTX, None, "shd"),
            P(GRP_CTX, None, "shd"),
            P(GRP_CTX, None, "shd"),
            P(GRP_CTX),
        ),
        out_specs=(
            P("grp", CTX, "shd"),
            P(None, "shd"),
            P("shd"),
            P(None, "shd"),
            P("shd"),
            P(GRP_CTX, None, "shd"),
            P(GRP_CTX, "shd", None, None),
        ),
        check_vma=False,
    )
```

```python
import jax
import jax.numpy as jnp
from jax import lax
from jax.experimental import pallas as pl
from jax.experimental.pallas import tpu as pltpu
from jax.sharding import Mesh
from jax.sharding import PartitionSpec as P

HEAD_DIM = 64
STATE = 128
INNER = 8192
STEPS = 4
CTX = ("far", "near", "ctx_1")
GRP_CTX = ("grp", "far", "near", "ctx_1")
GROUP = ("near", "ctx_1")

F32 = jnp.float32
BF16 = jnp.bfloat16
HIGHEST = lax.Precision.HIGHEST
EPSILON = 1e-05
KEEP_SHARE = 0.75
STEP_RATE = 0.001

TOKENS = 256
HEADS = 16
UNITS = 1024
SLABS = 8
MEMBERS = 8
FAR = 4
NEVER = -1e30


def call(body, outs, *args, smem=(), vmem=None, after=(), hbm=(), scratch=()):
    specs = [
        pl.BlockSpec(
            memory_space=pltpu.SMEM if i in smem else pltpu.HBM if i in hbm else pltpu.VMEM
        )
        for i in range(len(args))
    ] + [pl.BlockSpec(memory_space=pl.ANY) for _ in after]

    def run(*refs):
        body(*refs[: len(args)], *refs[len(args) + len(after) :])

    return pl.pallas_call(
        run,
        out_shape=[jax.ShapeDtypeStruct(shape, dtype) for shape, dtype in outs],
        in_specs=specs,
        out_specs=[pl.BlockSpec(memory_space=pltpu.VMEM) for _ in outs],
        scratch_shapes=list(scratch),
        compiler_params=pltpu.CompilerParams(vmem_limit_bytes=vmem or 24 * 2**20),
    )(*args, *after)


def dot(a, b, over, precision=None):
    return lax.dot_general(
        a, b, (((over[0],), (over[1],)), ((), ())), precision=precision, preferred_element_type=F32
    )


def halves(a):
    top = a.astype(BF16)
    return top, (a - top.astype(F32)).astype(BF16)


def dot_left(a, b, over):
    top, rest = halves(a)
    return dot(top, b, over) + dot(rest, b, over)


def dot_right(a, b, over):
    top, rest = halves(b)
    return dot(a, top, over) + dot(a, rest, over)


def iota(shape, dim):
    return lax.broadcasted_iota(jnp.int32, shape, dim)


def first_head(rows):
    return iota((rows, 128), 1) < HEAD_DIM


def of_pair(table, slab):
    left = jnp.broadcast_to(table[:, 2 * slab : 2 * slab + 1], (table.shape[0], 128))
    right = jnp.broadcast_to(table[:, 2 * slab + 1 : 2 * slab + 2], (table.shape[0], 128))
    return jnp.where(first_head(table.shape[0]), left, right)


def head_mask(slab):
    return (iota((HEADS, 128), 0) == 2 * slab + iota((HEADS, 128), 1) // HEAD_DIM).astype(BF16)


def units(slab):
    return slice(128 * slab, 128 * slab + 128)


def silu(g):
    return g * (1.0 / (1.0 + jnp.exp(-g)))


def softplus(z):
    return jnp.maximum(z, 0.0) + jnp.log1p(jnp.exp(-jnp.abs(z)))


def sigmoid(z):
    return 1.0 / (1.0 + jnp.exp(-z))


def column(heads, row):
    same = iota((HEADS, HEADS), 0) == iota((HEADS, HEADS), 1)
    return jnp.sum(jnp.where(same, heads[row : row + 1, :], 0.0), axis=1, keepdims=True)


def fetch(sources, targets, sems):
    copies = [
        pltpu.make_async_copy(source, target, sems.at[i])
        for i, (source, target) in enumerate(zip(sources, targets))
    ]
    for copy in copies:
        copy.start()
    return copies


def state_body(
    x_far, b_far, raw_far, heads_far, send, cum_out, turned, rates, x, b, raw, heads, sems
):
    copies = fetch((heads_far, raw_far, b_far, x_far), (heads, raw, b, x), sems)
    copies[0].wait()
    copies[1].wait()
    z = raw[...] + column(heads, 1)
    step = softplus(z)
    slope = sigmoid(z)
    rate = jnp.exp(column(heads, 0))
    log_decay = -rate * step
    upper = (iota((TOKENS, TOKENS), 0) <= iota((TOKENS, TOKENS), 1)).astype(F32)
    both = dot(jnp.concatenate([log_decay, slope], axis=0), upper, (1, 0), HIGHEST)
    cum = both[0:HEADS]
    cum_slope = both[HEADS:]
    last = cum[:, TOKENS - 1 : TOKENS]
    last_slope = -rate * cum_slope[:, TOKENS - 1 : TOKENS]
    tail = (jnp.exp(last - cum) * step).T
    copies[2].wait()
    copies[3].wait()
    writes = b[...]
    for slab in range(SLABS):
        scaled = x[:, units(slab)].astype(F32) * of_pair(tail, slab)
        send[slab, 0:128, :] = dot_left(scaled, writes, (0, 0))
        for i in range(2):
            h = 2 * slab + i
            send[slab, 128 + i : 129 + i, :] = jnp.broadcast_to(last[h : h + 1, :], (1, 128))
            send[slab, 130 + i : 131 + i, :] = jnp.broadcast_to(last_slope[h : h + 1, :], (1, 128))
        send[slab, 132:136, :] = jnp.zeros((4, 128), F32)
    turned[0] = cum
    turned[1] = cum_slope
    turned[2] = step
    turned[3] = slope
    cum_out[0] = cum.T
    cum_out[1] = cum_slope.T
    rates[...] = jnp.broadcast_to(rate, (HEADS, 128))


def tangent_body(x, b, turned, rates, send):
    writes = b[...]
    cum, cum_slope, step, slope = (turned[i] for i in range(4))
    rate = rates[:, 0:1]
    spread = cum[:, TOKENS - 1 : TOKENS] - cum
    spread_slope = rate * (cum_slope - cum_slope[:, TOKENS - 1 : TOKENS])
    kept = jnp.exp(spread)
    tangents = (
        (spread * kept * step).T,
        (kept * slope + spread_slope * kept * step).T,
    )
    for slab in range(SLABS):
        values = x[:, units(slab)].astype(F32)
        for i in range(2):
            scaled = values * of_pair(tangents[i], slab)
            send[slab, 128 * i : 128 * i + 128, :] = dot_left(scaled, writes, (0, 0))


def of_rows(pair):
    return jnp.concatenate(
        [jnp.broadcast_to(pair[0:1, :], (64, 128)), jnp.broadcast_to(pair[1:2, :], (64, 128))], axis=0
    )


def kept_rows(pair):
    return of_rows(jnp.exp(pair[0:2, :]))


def group_body(got, decays, total):
    state = got[0, 0:128, :]
    whole = got[0, 128:136, :]
    decays[0] = whole
    for k in range(1, MEMBERS):
        pair = got[k, 128:136, :]
        decays[k] = pair
        state = kept_rows(pair) * state + got[k, 0:128, :]
        whole = whole + pair
    total[0:128, :] = state
    total[128:136, :] = whole


def from_groups(three, two, one):
    state = three[0:128, :]
    for group in (two, one):
        state = kept_rows(group[128:136, :]) * state + group[0:128, :]
    return state


def later_group_body(decays, got, total):
    state = got[MEMBERS - 1]
    whole = decays[MEMBERS - 1]
    for k in reversed(range(MEMBERS - 1)):
        pair = decays[k]
        state = kept_rows(pair) * state + got[k]
        whole = whole + pair
    total[0:128, :] = state
    total[128:136, :] = whole


def earlier_body(got, three, two, one, back):
    state = from_groups(three, two, one)
    for k in range(MEMBERS):
        back[k] = state
        if k < MEMBERS - 1:
            state = kept_rows(got[k, 128:136, :]) * state + got[k, 0:128, :]


def tangent_scan_body(decays, states, tangents, scanned, total):
    rate = jnp.zeros((128, 128), F32)
    bias = jnp.zeros((128, 128), F32)
    for k in range(MEMBERS):
        scanned[k, 0:128, :] = rate
        scanned[k, 128:256, :] = bias
        pair = decays[k]
        keep = kept_rows(pair)
        kept = keep * states[k]
        rate = keep * rate + tangents[k, 0:128, :] + of_rows(pair) * kept
        bias = keep * bias + tangents[k, 128:256, :] + of_rows(pair[2:4, :]) * kept
    total[0:128, :] = rate
    total[128:256, :] = bias


def causal():
    return iota((TOKENS, TOKENS), 0) >= iota((TOKENS, TOKENS), 1)


def inside_body(x, b, c, cum, turned, heads, out):
    scores = dot(c[...], b[...], (1, 1))
    mask = causal()
    left = first_head(TOKENS)
    for slab in range(SLABS):
        values = x[:, units(slab)]
        parts = []
        for h in (2 * slab, 2 * slab + 1):
            spread = cum[0, :, h : h + 1] - turned[0, h : h + 1, :]
            weights = jnp.exp(jnp.where(mask, spread, NEVER)) * turned[2, h : h + 1, :]
            parts.append(dot_left(scores * weights, values, (1, 0)))
        skip = of_pair(heads[2:3, :], slab)
        out[:, units(slab)] = jnp.where(left, parts[0], parts[1]) + skip * values.astype(F32)


def mixed_body(inside, state, c, cum, gates, cotangent, gain, carried, sums):
    reads = c[...]
    carry = jnp.exp(cum[0])
    squares = jnp.zeros((TOKENS, 128), F32)
    products = jnp.zeros((TOKENS, 128), F32)
    for slab in range(SLABS):
        part = dot_right(reads, state[units(slab), :], (1, 1)) * of_pair(carry, slab)
        carried[:, units(slab)] = part
        gated = (inside[:, units(slab)] + part) * silu(gates[:, units(slab)].astype(F32))
        squares = squares + gated * gated
        products = products + cotangent[:, units(slab)].astype(F32) * gain[:, units(slab)] * gated
    ones = jnp.ones((8, 128), F32)
    squares = dot(ones, squares, (1, 1), HIGHEST)
    products = dot(ones, products, (1, 1), HIGHEST)
    both = jnp.concatenate(
        [
            squares[0:1, 0:128],
            squares[0:1, 128:256],
            products[0:1, 0:128],
            products[0:1, 128:256],
            jnp.zeros((4, 128), F32),
        ],
        axis=0,
    )
    for k in range(8):
        sums[k] = both


def spread_sum(flat, first):
    row = iota((64, 128), 0) % 8
    return jnp.concatenate(
        [dot(flat, (row == first + i).astype(F32), (0, 0), HIGHEST) for i in range(2)], axis=0
    )


def slope_body(c, cum, gates, cotangent, gain, inside, carried, sums, seq_out, slopes, send, gains):
    flat = sums[...].reshape(64, 128)
    squares = spread_sum(flat, 0)
    products = spread_sum(flat, 2)
    inverse = lax.rsqrt(squares / INNER + EPSILON)
    pull = inverse * inverse * inverse * products / INNER
    carry = jnp.exp(cum[0])
    reads = c[...]
    for slab in range(SLABS):
        act = silu(gates[:, units(slab)].astype(F32))
        gated = (inside[:, units(slab)] + carried[:, units(slab)]) * act
        normed = gated * inverse
        weight = gain[:, units(slab)]
        cot = cotangent[:, units(slab)].astype(F32)
        seq_out[:, units(slab)] = (normed * weight).astype(BF16)
        gain_slope = jnp.sum(cot * normed, axis=0, keepdims=True)
        mixed_slope = (cot * weight * inverse - gated * pull) * act
        slopes[:, units(slab)] = mixed_slope
        send[slab] = dot_left(mixed_slope * of_pair(carry, slab), reads, (0, 0))
        gains[slab : slab + 1, :] = gain_slope


def back_body(x, b, c, cum, turned, slopes, carried, out):
    scores = dot(c[...], b[...], (1, 1))
    mask = causal()
    left = first_head(TOKENS)
    carried_sum = jnp.zeros((HEADS, TOKENS), F32)
    skip_sum = jnp.zeros((HEADS, TOKENS), F32)
    for slab in range(SLABS):
        values = x[:, units(slab)]
        slope = slopes[:, units(slab)]
        member = head_mask(slab)
        carried_sum = carried_sum + dot_right(member, slope * carried[:, units(slab)], (1, 1))
        skip_sum = skip_sum + dot_right(member, slope * values.astype(F32), (1, 1))
        top, rest = halves(slope)
        for i in range(2):
            h = 2 * slab + i
            own = left if i == 0 else jnp.logical_not(left)
            value_h = jnp.where(own, values.astype(F32), 0.0).astype(BF16)
            product = dot(top, value_h, (1, 1)) + dot(rest, value_h, (1, 1))
            spread = cum[0, :, h : h + 1] - turned[0, h : h + 1, :]
            weights = jnp.exp(jnp.where(mask, spread, NEVER)) * turned[2, h : h + 1, :]
            each = product * scores * weights
            spread_slope = cum[1, :, h : h + 1] - turned[1, h : h + 1, :]
            out[0, h : h + 1, :] = jnp.sum(each, axis=0, keepdims=True)
            out[1, h : h + 1, :] = jnp.sum(each * spread, axis=0, keepdims=True)
            out[2, h : h + 1, :] = jnp.sum(each * spread_slope, axis=0, keepdims=True)
    out[3] = carried_sum
    out[4] = skip_sum


def meet_body(got, scanned, out):
    for i in range(2):
        met = got[0] * scanned[0, 128 * i : 128 * i + 128, :]
        for k in range(1, MEMBERS):
            met = met + got[k] * scanned[k, 128 * i : 128 * i + 128, :]
        out[128 * i : 128 * i + 128, :] = met


def heads_body(place, met, tangents, three, two, one, turned, inner, heads, gains, send):
    later = from_groups(three, two, one)
    rate_sum = met[0:128, :] + later * tangents[0:128, :]
    bias_sum = met[128:256, :] + later * tangents[128:256, :]

    def total(a):
        return jnp.sum(a, axis=1, keepdims=True)

    cum, cum_slope, step, slope = (turned[i] for i in range(4))
    carried = inner[3]
    rate_slope = total(inner[1] + carried * cum)
    bias_slope = total(inner[0] * slope / step) - jnp.exp(column(heads, 0)) * total(
        inner[2] + carried * cum_slope
    )
    skip_slope = total(inner[4])
    row = iota((HEADS, 1), 0)
    for i in range(2):
        own = row == 2 * place[0] + i
        half = slice(64 * i, 64 * i + 64)
        rate_slope = rate_slope + jnp.where(own, total(jnp.sum(rate_sum[half], axis=0, keepdims=True)), 0.0)
        bias_slope = bias_slope + jnp.where(own, total(jnp.sum(bias_sum[half], axis=0, keepdims=True)), 0.0)
    lane = iota((HEADS, 8), 1)
    table = jnp.where(
        lane == 0, rate_slope, jnp.where(lane == 1, bias_slope, jnp.where(lane == 2, skip_slope, 0.0))
    )
    unit = (iota((HEADS, 128), 0) == iota((HEADS, 128), 1)).astype(F32)
    rows = dot(table, unit, (0, 0), HIGHEST)
    for k in range(4):
        for i in range(3):
            send[k, :, 128 * i : 128 * i + 128] = rows[i : i + 1, :]
        for slab in range(SLABS):
            send[k, :, 384 + 128 * slab : 512 + 128 * slab] = gains[slab : slab + 1, :]


def near_body(got, send):
    row = got[0] + got[1] + got[2] + got[3]
    for k in range(16):
        send[k] = row


def before_body(state, reads, writes, out):
    for r in range(2):
        out[r, 0:4, :] = dot(reads[r], state[r], (1, 1))
        meet = dot(writes[r], reads[r], (1, 1))
        out[r, 4:8, 0:128] = jnp.concatenate([meet, jnp.zeros((4, 124), F32)], axis=1)


def decode_body(
    lengths, got, heads, slow, raw, values, gates, before, gated_out, sums, weights_out, gains,
    head_sum, blended,
):
    total = got[0]
    for k in range(1, 16):
        total = total + got[k]
    for slab in range(SLABS):
        gains[slab : slab + 1, :] = total[:, 384 + 128 * slab : 512 + 128 * slab]
    total = jnp.concatenate([total[:, 128 * i : 128 * i + HEADS] for i in range(3)], axis=0)
    head_sum[...] = total
    blend = KEEP_SHARE * slow[...] + (1.0 - KEEP_SHARE) * (heads[...] - STEP_RATE * total)
    blended[...] = blend
    step = softplus(raw[...] + blend[1:2, :])
    log_decay = -jnp.exp(blend[0:1, :]) * step
    spread = (iota((HEADS, UNITS), 0) == iota((HEADS, UNITS), 1) // HEAD_DIM).astype(F32)
    table = jnp.concatenate([step, log_decay, jnp.broadcast_to(blend[2:3, :], (8, HEADS))], axis=0)
    wide = dot(table, spread, (1, 0), HIGHEST)
    skip = wide[16:17, :]
    row8 = iota((8, 128), 0)
    totals = jnp.zeros((8, 128), F32)
    for r in range(2):
        length = lengths[r]
        cum = []
        drive = []
        rows = values[r].astype(F32)
        for k in range(STEPS):
            at = 4 * r + k
            log_k = wide[8 + at : 9 + at, :]
            cum.append(log_k if k == 0 else cum[-1] + log_k)
            drive.append(wide[at : at + 1, :] * rows[k : k + 1, :])
        act = silu(gates[r].astype(F32))
        for k in range(STEPS):
            read = jnp.exp(cum[k]) * before[r, k : k + 1, :] + skip * rows[k : k + 1, :]
            for j in range(k + 1):
                kept = drive[j] if j == k else jnp.exp(cum[k] - cum[j]) * drive[j]
                read = read + kept * before[r, 4 + j : 5 + j, k : k + 1]
            gated = read * act[k : k + 1, :]
            gated_out[r, k : k + 1, :] = gated
            squares = jnp.sum(gated * gated, axis=1, keepdims=True)
            totals = jnp.where(row8 == 4 * r + k, squares, totals)
        end = cum[0]
        for k in range(1, STEPS):
            end = jnp.where(length > k, cum[k], end)
        weights = [jnp.exp(end)]
        for j in range(STEPS):
            live = length > j
            weights.append(jnp.where(live, jnp.exp(jnp.where(live, end - cum[j], 0.0)) * drive[j], 0.0))
        weights.append(jnp.zeros((3, UNITS), F32))
        weights_out[r] = jnp.concatenate(weights, axis=0)
    for k in range(8):
        sums[k] = totals


def final_body(weights, writes, state, final):
    first = (iota((8, STATE), 0) == 0).astype(F32)
    for r in range(2):
        wide_writes = jnp.concatenate(
            [jnp.zeros((1, STATE), F32), writes[r].astype(F32), jnp.zeros((3, STATE), F32)], axis=0
        )
        kept = dot(weights[r], first, (0, 0), HIGHEST)
        fresh = dot(weights[r], wide_writes, (0, 0), HIGHEST)
        final[r] = kept * state[r].astype(F32) + fresh


def rows_body(lengths, got, gated, gain, gain_slope, slow, out, gain_out):
    blend = KEEP_SHARE * slow[...] + (1.0 - KEEP_SHARE) * (gain[...] - STEP_RATE * gain_slope[...])
    gain_out[...] = blend
    total = got[0]
    for k in range(1, 8):
        total = total + got[k]
    inverse = lax.rsqrt(total / INNER + EPSILON)
    for slab in range(SLABS):
        for r in range(2):
            shown = gated[r, :, units(slab)] * inverse[4 * r : 4 * r + 4, :] * blend[slab : slab + 1, :]
            live = iota((STEPS, 128), 0) < lengths[r]
            out[r, :, units(slab)] = jnp.where(live, shown, 0.0).astype(BF16)


def exchange(value, axes):
    return lax.all_to_all(value, axes, split_axis=0, concat_axis=0, tiled=True)


def shifted(value, by):
    pairs = [(k, k + by) for k in range(FAR) if 0 <= k + by < FAR]
    return lax.ppermute(value, "far", pairs)


def on_device(
    train_values,
    train_gates,
    train_writes,
    train_reads,
    train_steps,
    out_cotangent,
    head_params,
    norm_gain,
    slow_heads,
    slow_gain,
    roll_state,
    roll_values,
    roll_gates,
    roll_writes,
    roll_reads,
    roll_steps,
    roll_lengths,
):
    x, gates, cotangent = train_values[0], train_gates[0], out_cotangent[0]
    b, c, raw = train_writes[0], train_reads[0], train_steps[0].T
    gain = norm_gain.reshape(1, UNITS)
    wide = (TOKENS, UNITS)
    group = (136, STATE)
    tile = (8, 8, 128)

    bound = lax.optimization_barrier
    send, cum, turned, rates = call(
        state_body,
        [
            ((MEMBERS, 136, STATE), F32),
            ((2, TOKENS, HEADS), F32),
            ((4, HEADS, TOKENS), F32),
            ((HEADS, 128), F32),
        ],
        x, b, raw, head_params,
        hbm=(0, 1, 2, 3),
        vmem=60 * 2**20,
        scratch=(
            pltpu.VMEM((TOKENS, UNITS), BF16),
            pltpu.VMEM((TOKENS, STATE), BF16),
            pltpu.VMEM((HEADS, TOKENS), F32),
            pltpu.VMEM((3, HEADS), F32),
            pltpu.SemaphoreType.DMA((4,)),
        ),
    )
    got = exchange(send, GROUP)
    (send,) = call(tangent_body, [((MEMBERS, 256, STATE), F32)], x, b, turned, rates)
    (inside,) = call(
        inside_body, [(wide, F32)], x, b, c, cum, turned, head_params, after=(gates, cotangent)
    )
    decays, total = call(group_body, [(tile, F32), (group, F32)], got)
    send, total = bound((send, total))
    tangents = exchange(send, GROUP)
    groups = [shifted(total, by) for by in (3, 2, 1)]
    (back,) = call(
        earlier_body, [((MEMBERS, 128, STATE), F32)], got, *groups, after=(tangents,)
    )
    state_in = exchange(back, GROUP).reshape(UNITS, STATE)
    scanned, group_tangents = call(
        tangent_scan_body,
        [((MEMBERS, 256, STATE), F32), ((256, STATE), F32)],
        decays, back, tangents,
    )
    carried, sums = call(
        mixed_body, [(wide, F32), (tile, F32)], inside, state_in, c, cum, gates, cotangent, gain
    )
    sums = exchange(sums, "shd")
    seq_out, slopes, send, gains = call(
        slope_body,
        [(wide, BF16), (wide, F32), ((MEMBERS, 128, STATE), F32), ((8, 128), F32)],
        c, cum, gates, cotangent, gain, inside, carried, sums,
    )
    upward = exchange(send, GROUP)
    (total,) = call(later_group_body, [(group, F32)], decays, upward)
    groups = [shifted(total, -by) for by in (3, 2, 1)]
    (met,) = call(meet_body, [((256, STATE), F32)], upward, scanned)
    (inner,) = call(
        back_body, [((5, HEADS, TOKENS), F32)], x, b, c, cum, turned, slopes, carried
    )
    flat_state = roll_state.reshape(2, UNITS, STATE)
    (before,) = call(before_body, [((2, 8, UNITS), F32)], flat_state, roll_reads, roll_writes)
    place = (2 * lax.axis_index("near") + lax.axis_index("ctx_1")).reshape(1)
    (send,) = call(
        heads_body,
        [((4, 1, 1408), F32)],
        place, met, group_tangents, *groups, turned, inner, head_params, gains,
        smem=(0,),
    )
    near = exchange(send, ("grp", "ctx_1"))
    (send,) = call(near_body, [((16, 1, 1408), F32)], near)
    far = exchange(send, ("far", "near"))
    gated, sums, weights, gain_slope, head_sum, blend_heads = call(
        decode_body,
        [
            ((2, STEPS, UNITS), F32),
            (tile, F32),
            ((2, 8, UNITS), F32),
            ((8, 128), F32),
            ((3, HEADS), F32),
            ((3, HEADS), F32),
        ],
        roll_lengths, far, head_params, slow_heads, roll_steps.reshape(8, HEADS), roll_values,
        roll_gates, before,
        smem=(0,),
    )
    sums = exchange(sums, "shd")
    (final,) = call(
        final_body, [((2, UNITS, STATE), F32)], weights, roll_writes, flat_state
    )
    roll_out, blend_gain = call(
        rows_body,
        [((2, STEPS, UNITS), BF16), ((8, 128), F32)],
        roll_lengths, sums, gated, norm_gain.reshape(8, 128), gain_slope, slow_gain.reshape(8, 128),
        smem=(0,),
    )
    return (
        seq_out[None],
        head_sum,
        gain_slope.reshape(UNITS),
        blend_heads,
        blend_gain.reshape(UNITS),
        roll_out,
        final.reshape(2, HEADS, HEAD_DIM, STATE),
    )


def solution(mesh):
    split = Mesh(
        mesh.devices.reshape(mesh.shape["grp"], FAR, 4, 2, mesh.shape["shd"]),
        ("grp", "far", "near", "ctx_1", "shd"),
    )
    return jax.shard_map(
        on_device,
        mesh=split,
        in_specs=(
            P("grp", CTX, "shd"),
            P("grp", CTX, "shd"),
            P("grp", CTX, "shd"),
            P("grp", CTX, "shd"),
            P("grp", CTX, "shd"),
            P("grp", CTX, "shd"),
            P(None, "shd"),
            P("shd"),
            P(None, "shd"),
            P("shd"),
            P(GRP_CTX, "shd", None, None),
            P(GRP_CTX, None, "shd"),
            P(GRP_CTX, None, "shd"),
            P(GRP_CTX, None, "shd"),
            P(GRP_CTX, None, "shd"),
            P(GRP_CTX, None, "shd"),
            P(GRP_CTX),
        ),
        out_specs=(
            P("grp", CTX, "shd"),
            P(None, "shd"),
            P("shd"),
            P(None, "shd"),
            P("shd"),
            P(GRP_CTX, None, "shd"),
            P(GRP_CTX, "shd", None, None),
        ),
        check_vma=False,
    )
```

```python
import jax
import jax.numpy as jnp
from jax import lax
from jax.experimental import pallas as pl
from jax.experimental.pallas import tpu as pltpu
from jax.sharding import Mesh
from jax.sharding import PartitionSpec as P

HEAD_DIM = 64
STATE = 128
INNER = 8192
STEPS = 4
CTX = ("far", "near", "ctx_1")
GRP_CTX = ("grp", "far", "near", "ctx_1")
GROUP = ("near", "ctx_1")

F32 = jnp.float32
BF16 = jnp.bfloat16
HIGHEST = lax.Precision.HIGHEST
EPSILON = 1e-05
KEEP_SHARE = 0.75
STEP_RATE = 0.001

TOKENS = 256
HEADS = 16
UNITS = 1024
SLABS = 8
MEMBERS = 8
FAR = 4
NEVER = -1e30


def call(body, outs, *args, smem=(), vmem=None, after=(), hbm=(), scratch=()):
    specs = [
        pl.BlockSpec(
            memory_space=pltpu.SMEM if i in smem else pltpu.HBM if i in hbm else pltpu.VMEM
        )
        for i in range(len(args))
    ] + [pl.BlockSpec(memory_space=pl.ANY) for _ in after]

    def run(*refs):
        body(*refs[: len(args)], *refs[len(args) + len(after) :])

    return pl.pallas_call(
        run,
        out_shape=[jax.ShapeDtypeStruct(shape, dtype) for shape, dtype in outs],
        in_specs=specs,
        out_specs=[pl.BlockSpec(memory_space=pltpu.VMEM) for _ in outs],
        scratch_shapes=list(scratch),
        compiler_params=pltpu.CompilerParams(vmem_limit_bytes=vmem or 10 * 2**20),
    )(*args, *after)


def dot(a, b, over, precision=None):
    return lax.dot_general(
        a, b, (((over[0],), (over[1],)), ((), ())), precision=precision, preferred_element_type=F32
    )


def halves(a):
    top = a.astype(BF16)
    return top, (a - top.astype(F32)).astype(BF16)


def dot_left(a, b, over):
    top, rest = halves(a)
    return dot(top, b, over) + dot(rest, b, over)


def dot_right(a, b, over):
    top, rest = halves(b)
    return dot(a, top, over) + dot(a, rest, over)


def iota(shape, dim):
    return lax.broadcasted_iota(jnp.int32, shape, dim)


def first_head(rows):
    return iota((rows, 128), 1) < HEAD_DIM


def of_pair(table, slab):
    left = jnp.broadcast_to(table[:, 2 * slab : 2 * slab + 1], (table.shape[0], 128))
    right = jnp.broadcast_to(table[:, 2 * slab + 1 : 2 * slab + 2], (table.shape[0], 128))
    return jnp.where(first_head(table.shape[0]), left, right)


def head_mask(slab):
    return (iota((HEADS, 128), 0) == 2 * slab + iota((HEADS, 128), 1) // HEAD_DIM).astype(BF16)


def units(slab):
    return slice(128 * slab, 128 * slab + 128)


def silu(g):
    return g * (1.0 / (1.0 + jnp.exp(-g)))


def softplus(z):
    return jnp.maximum(z, 0.0) + jnp.log1p(jnp.exp(-jnp.abs(z)))


def sigmoid(z):
    return 1.0 / (1.0 + jnp.exp(-z))


def column(heads, row):
    same = iota((HEADS, HEADS), 0) == iota((HEADS, HEADS), 1)
    return jnp.sum(jnp.where(same, heads[row : row + 1, :], 0.0), axis=1, keepdims=True)


def fetch(sources, targets, sems):
    copies = [
        pltpu.make_async_copy(source, target, sems.at[i])
        for i, (source, target) in enumerate(zip(sources, targets))
    ]
    for copy in copies:
        copy.start()
    return copies


def state_body(
    x_far, b_far, raw_far, heads_far, send, cum_out, turned, rates, x, b, raw, heads, sems
):
    copies = fetch((heads_far, raw_far, b_far, x_far), (heads, raw, b, x), sems)
    copies[0].wait()
    copies[1].wait()
    z = raw[...] + column(heads, 1)
    step = softplus(z)
    slope = sigmoid(z)
    rate = jnp.exp(column(heads, 0))
    log_decay = -rate * step
    upper = (iota((TOKENS, TOKENS), 0) <= iota((TOKENS, TOKENS), 1)).astype(F32)
    both = dot(jnp.concatenate([log_decay, slope], axis=0), upper, (1, 0), HIGHEST)
    cum = both[0:HEADS]
    cum_slope = both[HEADS:]
    last = cum[:, TOKENS - 1 : TOKENS]
    last_slope = -rate * cum_slope[:, TOKENS - 1 : TOKENS]
    tail = (jnp.exp(last - cum) * step).T
    copies[2].wait()
    copies[3].wait()
    writes = b[...]
    for slab in range(SLABS):
        scaled = x[:, units(slab)].astype(F32) * of_pair(tail, slab)
        send[slab, 0:128, :] = dot_left(scaled, writes, (0, 0))
        for i in range(2):
            h = 2 * slab + i
            send[slab, 128 + i : 129 + i, :] = jnp.broadcast_to(last[h : h + 1, :], (1, 128))
            send[slab, 130 + i : 131 + i, :] = jnp.broadcast_to(last_slope[h : h + 1, :], (1, 128))
        send[slab, 132:136, :] = jnp.zeros((4, 128), F32)
    turned[0] = cum
    turned[1] = cum_slope
    turned[2] = step
    turned[3] = slope
    cum_out[0] = cum.T
    cum_out[1] = cum_slope.T
    rates[...] = jnp.broadcast_to(rate, (HEADS, 128))


def tangent_body(x, b, turned, rates, send):
    writes = b[...]
    cum, cum_slope, step, slope = (turned[i] for i in range(4))
    rate = rates[:, 0:1]
    spread = cum[:, TOKENS - 1 : TOKENS] - cum
    spread_slope = rate * (cum_slope - cum_slope[:, TOKENS - 1 : TOKENS])
    kept = jnp.exp(spread)
    tangents = (
        (spread * kept * step).T,
        (kept * slope + spread_slope * kept * step).T,
    )
    for slab in range(SLABS):
        values = x[:, units(slab)].astype(F32)
        for i in range(2):
            scaled = values * of_pair(tangents[i], slab)
            send[slab, 128 * i : 128 * i + 128, :] = dot_left(scaled, writes, (0, 0))


def of_rows(pair):
    return jnp.concatenate(
        [jnp.broadcast_to(pair[0:1, :], (64, 128)), jnp.broadcast_to(pair[1:2, :], (64, 128))], axis=0
    )


def kept_rows(pair):
    return of_rows(jnp.exp(pair[0:2, :]))


def group_body(got, total):
    state = got[0, 0:128, :]
    whole = got[0, 128:136, :]
    for k in range(1, MEMBERS):
        pair = got[k, 128:136, :]
        state = kept_rows(pair) * state + got[k, 0:128, :]
        whole = whole + pair
    total[0:128, :] = state
    total[128:136, :] = whole


def from_groups(three, two, one):
    state = three[0:128, :]
    for group in (two, one):
        state = kept_rows(group[128:136, :]) * state + group[0:128, :]
    return state


def later_group_body(decays, got, total):
    state = got[MEMBERS - 1]
    whole = decays[MEMBERS - 1]
    for k in reversed(range(MEMBERS - 1)):
        pair = decays[k]
        state = kept_rows(pair) * state + got[k]
        whole = whole + pair
    total[0:128, :] = state
    total[128:136, :] = whole


def earlier_body(got, three, two, one, back):
    state = from_groups(three, two, one)
    for k in range(MEMBERS):
        back[k] = state
        if k < MEMBERS - 1:
            state = kept_rows(got[k, 128:136, :]) * state + got[k, 0:128, :]


def tangent_scan_body(got, states, tangents, scanned, total, decays):
    rate = jnp.zeros((128, 128), F32)
    bias = jnp.zeros((128, 128), F32)
    for k in range(MEMBERS):
        scanned[k, 0:128, :] = rate
        scanned[k, 128:256, :] = bias
        pair = got[k, 128:136, :]
        decays[k] = pair
        keep = kept_rows(pair)
        kept = keep * states[k]
        rate = keep * rate + tangents[k, 0:128, :] + of_rows(pair) * kept
        bias = keep * bias + tangents[k, 128:256, :] + of_rows(pair[2:4, :]) * kept
    total[0:128, :] = rate
    total[128:256, :] = bias


def causal():
    return iota((TOKENS, TOKENS), 0) >= iota((TOKENS, TOKENS), 1)


def inside_body(x, b, c, cum, turned, heads, out):
    scores = dot(c[...], b[...], (1, 1))
    mask = causal()
    left = first_head(TOKENS)
    for slab in range(SLABS):
        values = x[:, units(slab)]
        parts = []
        for h in (2 * slab, 2 * slab + 1):
            spread = cum[0, :, h : h + 1] - turned[0, h : h + 1, :]
            weights = jnp.exp(jnp.where(mask, spread, NEVER)) * turned[2, h : h + 1, :]
            parts.append(dot_left(scores * weights, values, (1, 0)))
        skip = of_pair(heads[2:3, :], slab)
        out[:, units(slab)] = jnp.where(left, parts[0], parts[1]) + skip * values.astype(F32)


def mixed_body(inside, state, c, cum, gates, cotangent, gain, carried, sums):
    reads = c[...]
    carry = jnp.exp(cum[0])
    squares = jnp.zeros((TOKENS, 128), F32)
    products = jnp.zeros((TOKENS, 128), F32)
    for slab in range(SLABS):
        part = dot_right(reads, state[units(slab), :], (1, 1)) * of_pair(carry, slab)
        carried[:, units(slab)] = part
        gated = (inside[:, units(slab)] + part) * silu(gates[:, units(slab)].astype(F32))
        squares = squares + gated * gated
        products = products + cotangent[:, units(slab)].astype(F32) * gain[:, units(slab)] * gated
    ones = jnp.ones((8, 128), F32)
    squares = dot(ones, squares, (1, 1), HIGHEST)
    products = dot(ones, products, (1, 1), HIGHEST)
    both = jnp.concatenate(
        [
            squares[0:1, 0:128],
            squares[0:1, 128:256],
            products[0:1, 0:128],
            products[0:1, 128:256],
            jnp.zeros((4, 128), F32),
        ],
        axis=0,
    )
    for k in range(8):
        sums[k] = both


def spread_sum(flat, first):
    row = iota((64, 128), 0) % 8
    return jnp.concatenate(
        [dot(flat, (row == first + i).astype(F32), (0, 0), HIGHEST) for i in range(2)], axis=0
    )


def slope_body(c, cum, gates, cotangent, gain, inside, carried, sums, seq_out, slopes, send, gains):
    flat = sums[...].reshape(64, 128)
    squares = spread_sum(flat, 0)
    products = spread_sum(flat, 2)
    inverse = lax.rsqrt(squares / INNER + EPSILON)
    pull = inverse * inverse * inverse * products / INNER
    carry = jnp.exp(cum[0])
    reads = c[...]
    for slab in range(SLABS):
        act = silu(gates[:, units(slab)].astype(F32))
        gated = (inside[:, units(slab)] + carried[:, units(slab)]) * act
        normed = gated * inverse
        weight = gain[:, units(slab)]
        cot = cotangent[:, units(slab)].astype(F32)
        seq_out[:, units(slab)] = (normed * weight).astype(BF16)
        gain_slope = jnp.sum(cot * normed, axis=0, keepdims=True)
        mixed_slope = (cot * weight * inverse - gated * pull) * act
        slopes[:, units(slab)] = mixed_slope
        send[slab] = dot_left(mixed_slope * of_pair(carry, slab), reads, (0, 0))
        gains[slab : slab + 1, :] = gain_slope


def back_body(x, b, c, cum, turned, slopes, carried, out):
    scores = dot(c[...], b[...], (1, 1))
    mask = causal()
    left = first_head(TOKENS)
    carried_sum = jnp.zeros((HEADS, TOKENS), F32)
    skip_sum = jnp.zeros((HEADS, TOKENS), F32)
    for slab in range(SLABS):
        values = x[:, units(slab)]
        slope = slopes[:, units(slab)]
        member = head_mask(slab)
        carried_sum = carried_sum + dot_right(member, slope * carried[:, units(slab)], (1, 1))
        skip_sum = skip_sum + dot_right(member, slope * values.astype(F32), (1, 1))
        top, rest = halves(slope)
        for i in range(2):
            h = 2 * slab + i
            own = left if i == 0 else jnp.logical_not(left)
            value_h = jnp.where(own, values.astype(F32), 0.0).astype(BF16)
            product = dot(top, value_h, (1, 1)) + dot(rest, value_h, (1, 1))
            spread = cum[0, :, h : h + 1] - turned[0, h : h + 1, :]
            weights = jnp.exp(jnp.where(mask, spread, NEVER)) * turned[2, h : h + 1, :]
            each = product * scores * weights
            spread_slope = cum[1, :, h : h + 1] - turned[1, h : h + 1, :]
            out[0, h : h + 1, :] = jnp.sum(each, axis=0, keepdims=True)
            out[1, h : h + 1, :] = jnp.sum(each * spread, axis=0, keepdims=True)
            out[2, h : h + 1, :] = jnp.sum(each * spread_slope, axis=0, keepdims=True)
    out[3] = carried_sum
    out[4] = skip_sum


def meet_body(got, scanned, out):
    for i in range(2):
        met = got[0] * scanned[0, 128 * i : 128 * i + 128, :]
        for k in range(1, MEMBERS):
            met = met + got[k] * scanned[k, 128 * i : 128 * i + 128, :]
        out[128 * i : 128 * i + 128, :] = met


def heads_body(place, met, tangents, three, two, one, turned, inner, heads, gains, send):
    later = from_groups(three, two, one)
    rate_sum = met[0:128, :] + later * tangents[0:128, :]
    bias_sum = met[128:256, :] + later * tangents[128:256, :]

    def total(a):
        return jnp.sum(a, axis=1, keepdims=True)

    cum, cum_slope, step, slope = (turned[i] for i in range(4))
    carried = inner[3]
    rate_slope = total(inner[1] + carried * cum)
    bias_slope = total(inner[0] * slope / step) - jnp.exp(column(heads, 0)) * total(
        inner[2] + carried * cum_slope
    )
    skip_slope = total(inner[4])
    row = iota((HEADS, 1), 0)
    for i in range(2):
        own = row == 2 * place[0] + i
        half = slice(64 * i, 64 * i + 64)
        rate_slope = rate_slope + jnp.where(own, total(jnp.sum(rate_sum[half], axis=0, keepdims=True)), 0.0)
        bias_slope = bias_slope + jnp.where(own, total(jnp.sum(bias_sum[half], axis=0, keepdims=True)), 0.0)
    lane = iota((HEADS, 8), 1)
    table = jnp.where(
        lane == 0, rate_slope, jnp.where(lane == 1, bias_slope, jnp.where(lane == 2, skip_slope, 0.0))
    )
    unit = (iota((HEADS, 128), 0) == iota((HEADS, 128), 1)).astype(F32)
    rows = dot(table, unit, (0, 0), HIGHEST)
    for k in range(4):
        for i in range(3):
            send[k, :, 128 * i : 128 * i + 128] = rows[i : i + 1, :]
        for slab in range(SLABS):
            send[k, :, 384 + 128 * slab : 512 + 128 * slab] = gains[slab : slab + 1, :]


def near_body(got, send):
    row = got[0] + got[1] + got[2] + got[3]
    for k in range(16):
        send[k] = row


def before_body(state, reads, writes, out):
    for r in range(2):
        out[r, 0:4, :] = dot(reads[r], state[r], (1, 1))
        meet = dot(writes[r], reads[r], (1, 1))
        out[r, 4:8, 0:128] = jnp.concatenate([meet, jnp.zeros((4, 124), F32)], axis=1)


def decode_body(
    lengths, got, heads, slow, raw, values, gates, before, gated_out, sums, weights_out, gains,
    head_sum, blended,
):
    total = got[0]
    for k in range(1, 16):
        total = total + got[k]
    for slab in range(SLABS):
        gains[slab : slab + 1, :] = total[:, 384 + 128 * slab : 512 + 128 * slab]
    total = jnp.concatenate([total[:, 128 * i : 128 * i + HEADS] for i in range(3)], axis=0)
    head_sum[...] = total
    blend = KEEP_SHARE * slow[...] + (1.0 - KEEP_SHARE) * (heads[...] - STEP_RATE * total)
    blended[...] = blend
    step = softplus(raw[...] + blend[1:2, :])
    log_decay = -jnp.exp(blend[0:1, :]) * step
    spread = (iota((HEADS, UNITS), 0) == iota((HEADS, UNITS), 1) // HEAD_DIM).astype(F32)
    table = jnp.concatenate([step, log_decay, jnp.broadcast_to(blend[2:3, :], (8, HEADS))], axis=0)
    wide = dot(table, spread, (1, 0), HIGHEST)
    skip = wide[16:17, :]
    row8 = iota((8, 128), 0)
    totals = jnp.zeros((8, 128), F32)
    for r in range(2):
        length = lengths[r]
        cum = []
        drive = []
        rows = values[r].astype(F32)
        for k in range(STEPS):
            at = 4 * r + k
            log_k = wide[8 + at : 9 + at, :]
            cum.append(log_k if k == 0 else cum[-1] + log_k)
            drive.append(wide[at : at + 1, :] * rows[k : k + 1, :])
        act = silu(gates[r].astype(F32))
        for k in range(STEPS):
            read = jnp.exp(cum[k]) * before[r, k : k + 1, :] + skip * rows[k : k + 1, :]
            for j in range(k + 1):
                kept = drive[j] if j == k else jnp.exp(cum[k] - cum[j]) * drive[j]
                read = read + kept * before[r, 4 + j : 5 + j, k : k + 1]
            gated = read * act[k : k + 1, :]
            gated_out[r, k : k + 1, :] = gated
            squares = jnp.sum(gated * gated, axis=1, keepdims=True)
            totals = jnp.where(row8 == 4 * r + k, squares, totals)
        end = cum[0]
        for k in range(1, STEPS):
            end = jnp.where(length > k, cum[k], end)
        weights = [jnp.exp(end)]
        for j in range(STEPS):
            live = length > j
            weights.append(jnp.where(live, jnp.exp(jnp.where(live, end - cum[j], 0.0)) * drive[j], 0.0))
        weights.append(jnp.zeros((3, UNITS), F32))
        weights_out[r] = jnp.concatenate(weights, axis=0)
    for k in range(8):
        sums[k] = totals


def final_body(weights, writes, state, final):
    first = (iota((8, STATE), 0) == 0).astype(F32)
    for r in range(2):
        wide_writes = jnp.concatenate(
            [jnp.zeros((1, STATE), F32), writes[r].astype(F32), jnp.zeros((3, STATE), F32)], axis=0
        )
        kept = dot(weights[r], first, (0, 0), HIGHEST)
        fresh = dot(weights[r], wide_writes, (0, 0), HIGHEST)
        final[r] = kept * state[r].astype(F32) + fresh


def rows_body(lengths, got, gated, gain, gain_slope, slow, out, gain_out):
    blend = KEEP_SHARE * slow[...] + (1.0 - KEEP_SHARE) * (gain[...] - STEP_RATE * gain_slope[...])
    gain_out[...] = blend
    total = got[0]
    for k in range(1, 8):
        total = total + got[k]
    inverse = lax.rsqrt(total / INNER + EPSILON)
    for slab in range(SLABS):
        for r in range(2):
            shown = gated[r, :, units(slab)] * inverse[4 * r : 4 * r + 4, :] * blend[slab : slab + 1, :]
            live = iota((STEPS, 128), 0) < lengths[r]
            out[r, :, units(slab)] = jnp.where(live, shown, 0.0).astype(BF16)


def exchange(value, axes):
    return lax.all_to_all(value, axes, split_axis=0, concat_axis=0, tiled=True)


def shifted(value, by):
    pairs = [(k, k + by) for k in range(FAR) if 0 <= k + by < FAR]
    return lax.ppermute(value, "far", pairs)


def on_device(
    train_values,
    train_gates,
    train_writes,
    train_reads,
    train_steps,
    out_cotangent,
    head_params,
    norm_gain,
    slow_heads,
    slow_gain,
    roll_state,
    roll_values,
    roll_gates,
    roll_writes,
    roll_reads,
    roll_steps,
    roll_lengths,
):
    x, gates, cotangent = train_values[0], train_gates[0], out_cotangent[0]
    b, c, raw = train_writes[0], train_reads[0], train_steps[0].T
    gain = norm_gain.reshape(1, UNITS)
    wide = (TOKENS, UNITS)
    group = (136, STATE)
    tile = (8, 8, 128)

    bound = lax.optimization_barrier
    send, cum, turned, rates = call(
        state_body,
        [
            ((MEMBERS, 136, STATE), F32),
            ((2, TOKENS, HEADS), F32),
            ((4, HEADS, TOKENS), F32),
            ((HEADS, 128), F32),
        ],
        x, b, raw, head_params,
        hbm=(0, 1, 2, 3),
        vmem=60 * 2**20,
        scratch=(
            pltpu.VMEM((TOKENS, UNITS), BF16),
            pltpu.VMEM((TOKENS, STATE), BF16),
            pltpu.VMEM((HEADS, TOKENS), F32),
            pltpu.VMEM((3, HEADS), F32),
            pltpu.SemaphoreType.DMA((4,)),
        ),
    )
    got = exchange(send, GROUP)
    (send,) = call(tangent_body, [((MEMBERS, 256, STATE), F32)], x, b, turned, rates)
    (inside,) = call(
        inside_body, [(wide, F32)], x, b, c, cum, turned, head_params, after=(gates, cotangent)
    )
    (total,) = call(group_body, [(group, F32)], got)
    send, total = bound((send, total))
    tangents = exchange(send, GROUP)
    groups = [shifted(total, by) for by in (3, 2, 1)]
    (back,) = call(
        earlier_body, [((MEMBERS, 128, STATE), F32)], got, *groups, after=(tangents,)
    )
    state_in = exchange(back, GROUP).reshape(UNITS, STATE)
    scanned, group_tangents, decays = call(
        tangent_scan_body,
        [((MEMBERS, 256, STATE), F32), ((256, STATE), F32), (tile, F32)],
        got, back, tangents,
    )
    carried, sums = call(
        mixed_body,
        [(wide, F32), (tile, F32)],
        inside, state_in, c, cum, gates, cotangent, gain,
        after=(decays,),
    )
    sums = exchange(sums, "shd")
    seq_out, slopes, send, gains = call(
        slope_body,
        [(wide, BF16), (wide, F32), ((MEMBERS, 128, STATE), F32), ((8, 128), F32)],
        c, cum, gates, cotangent, gain, inside, carried, sums,
    )
    upward = exchange(send, GROUP)
    (total,) = call(later_group_body, [(group, F32)], decays, upward)
    groups = [shifted(total, -by) for by in (3, 2, 1)]
    (met,) = call(meet_body, [((256, STATE), F32)], upward, scanned)
    (inner,) = call(
        back_body, [((5, HEADS, TOKENS), F32)], x, b, c, cum, turned, slopes, carried
    )
    flat_state = roll_state.reshape(2, UNITS, STATE)
    (before,) = call(before_body, [((2, 8, UNITS), F32)], flat_state, roll_reads, roll_writes)
    place = (2 * lax.axis_index("near") + lax.axis_index("ctx_1")).reshape(1)
    (send,) = call(
        heads_body,
        [((4, 1, 1408), F32)],
        place, met, group_tangents, *groups, turned, inner, head_params, gains,
        smem=(0,),
    )
    near = exchange(send, ("grp", "ctx_1"))
    (send,) = call(near_body, [((16, 1, 1408), F32)], near)
    far = exchange(send, ("far", "near"))
    gated, sums, weights, gain_slope, head_sum, blend_heads = call(
        decode_body,
        [
            ((2, STEPS, UNITS), F32),
            (tile, F32),
            ((2, 8, UNITS), F32),
            ((8, 128), F32),
            ((3, HEADS), F32),
            ((3, HEADS), F32),
        ],
        roll_lengths, far, head_params, slow_heads, roll_steps.reshape(8, HEADS), roll_values,
        roll_gates, before,
        smem=(0,),
    )
    sums = exchange(sums, "shd")
    (final,) = call(
        final_body, [((2, UNITS, STATE), F32)], weights, roll_writes, flat_state
    )
    roll_out, blend_gain = call(
        rows_body,
        [((2, STEPS, UNITS), BF16), ((8, 128), F32)],
        roll_lengths, sums, gated, norm_gain.reshape(8, 128), gain_slope, slow_gain.reshape(8, 128),
        smem=(0,),
    )
    return (
        seq_out[None],
        head_sum,
        gain_slope.reshape(UNITS),
        blend_heads,
        blend_gain.reshape(UNITS),
        roll_out,
        final.reshape(2, HEADS, HEAD_DIM, STATE),
    )


def solution(mesh):
    split = Mesh(
        mesh.devices.reshape(mesh.shape["grp"], FAR, 4, 2, mesh.shape["shd"]),
        ("grp", "far", "near", "ctx_1", "shd"),
    )
    return jax.shard_map(
        on_device,
        mesh=split,
        in_specs=(
            P("grp", CTX, "shd"),
            P("grp", CTX, "shd"),
            P("grp", CTX, "shd"),
            P("grp", CTX, "shd"),
            P("grp", CTX, "shd"),
            P("grp", CTX, "shd"),
            P(None, "shd"),
            P("shd"),
            P(None, "shd"),
            P("shd"),
            P(GRP_CTX, "shd", None, None),
            P(GRP_CTX, None, "shd"),
            P(GRP_CTX, None, "shd"),
            P(GRP_CTX, None, "shd"),
            P(GRP_CTX, None, "shd"),
            P(GRP_CTX, None, "shd"),
            P(GRP_CTX),
        ),
        out_specs=(
            P("grp", CTX, "shd"),
            P(None, "shd"),
            P("shd"),
            P(None, "shd"),
            P("shd"),
            P(GRP_CTX, None, "shd"),
            P(GRP_CTX, "shd", None, None),
        ),
        check_vma=False,
    )
```

```python
import jax
import jax.numpy as jnp
from jax import lax
from jax.experimental import pallas as pl
from jax.experimental.pallas import tpu as pltpu
from jax.sharding import Mesh
from jax.sharding import PartitionSpec as P

HEAD_DIM = 64
STATE = 128
INNER = 8192
STEPS = 4
CTX = ("far", "near", "ctx_1")
GRP_CTX = ("grp", "far", "near", "ctx_1")
GROUP = ("near", "ctx_1")

F32 = jnp.float32
BF16 = jnp.bfloat16
HIGHEST = lax.Precision.HIGHEST
EPSILON = 1e-05
KEEP_SHARE = 0.75
STEP_RATE = 0.001

TOKENS = 256
HEADS = 16
UNITS = 1024
SLABS = 8
MEMBERS = 8
FAR = 4
NEVER = -1e30


def call(body, outs, *args, smem=(), vmem=None, after=(), hbm=(), scratch=()):
    specs = [
        pl.BlockSpec(
            memory_space=pltpu.SMEM if i in smem else pltpu.HBM if i in hbm else pltpu.VMEM
        )
        for i in range(len(args))
    ] + [pl.BlockSpec(memory_space=pl.ANY) for _ in after]

    def run(*refs):
        body(*refs[: len(args)], *refs[len(args) + len(after) :])

    return pl.pallas_call(
        run,
        out_shape=[jax.ShapeDtypeStruct(shape, dtype) for shape, dtype in outs],
        in_specs=specs,
        out_specs=[pl.BlockSpec(memory_space=pltpu.VMEM) for _ in outs],
        scratch_shapes=list(scratch),
        compiler_params=pltpu.CompilerParams(vmem_limit_bytes=vmem or 24 * 2**20),
    )(*args, *after)


def dot(a, b, over, precision=None):
    return lax.dot_general(
        a, b, (((over[0],), (over[1],)), ((), ())), precision=precision, preferred_element_type=F32
    )


def halves(a):
    top = a.astype(BF16)
    return top, (a - top.astype(F32)).astype(BF16)


def dot_left(a, b, over):
    top, rest = halves(a)
    return dot(top, b, over) + dot(rest, b, over)


def dot_right(a, b, over):
    top, rest = halves(b)
    return dot(a, top, over) + dot(a, rest, over)


def iota(shape, dim):
    return lax.broadcasted_iota(jnp.int32, shape, dim)


def first_head(rows):
    return iota((rows, 128), 1) < HEAD_DIM


def of_pair(table, slab):
    left = jnp.broadcast_to(table[:, 2 * slab : 2 * slab + 1], (table.shape[0], 128))
    right = jnp.broadcast_to(table[:, 2 * slab + 1 : 2 * slab + 2], (table.shape[0], 128))
    return jnp.where(first_head(table.shape[0]), left, right)


def head_mask(slab):
    return (iota((HEADS, 128), 0) == 2 * slab + iota((HEADS, 128), 1) // HEAD_DIM).astype(BF16)


def units(slab):
    return slice(128 * slab, 128 * slab + 128)


def silu(g):
    return g * (1.0 / (1.0 + jnp.exp(-g)))


def softplus(z):
    return jnp.maximum(z, 0.0) + jnp.log1p(jnp.exp(-jnp.abs(z)))


def sigmoid(z):
    return 1.0 / (1.0 + jnp.exp(-z))


def column(heads, row):
    same = iota((HEADS, HEADS), 0) == iota((HEADS, HEADS), 1)
    return jnp.sum(jnp.where(same, heads[row : row + 1, :], 0.0), axis=1, keepdims=True)


def fetch(sources, targets, sems):
    copies = [
        pltpu.make_async_copy(source, target, sems.at[i])
        for i, (source, target) in enumerate(zip(sources, targets))
    ]
    for copy in copies:
        copy.start()
    return copies


def state_body(
    x_far, b_far, raw_far, heads_far, send, cum_out, turned, rates, x, b, raw, heads, sems
):
    copies = fetch((heads_far, raw_far, b_far, x_far), (heads, raw, b, x), sems)
    copies[0].wait()
    copies[1].wait()
    z = raw[...] + column(heads, 1)
    step = softplus(z)
    slope = sigmoid(z)
    rate = jnp.exp(column(heads, 0))
    log_decay = -rate * step
    upper = (iota((TOKENS, TOKENS), 0) <= iota((TOKENS, TOKENS), 1)).astype(F32)
    both = dot(jnp.concatenate([log_decay, slope], axis=0), upper, (1, 0), HIGHEST)
    cum = both[0:HEADS]
    cum_slope = both[HEADS:]
    last = cum[:, TOKENS - 1 : TOKENS]
    last_slope = -rate * cum_slope[:, TOKENS - 1 : TOKENS]
    tail = (jnp.exp(last - cum) * step).T
    copies[2].wait()
    copies[3].wait()
    writes = b[...]
    for slab in range(SLABS):
        scaled = x[:, units(slab)].astype(F32) * of_pair(tail, slab)
        send[slab, 0:128, :] = dot_left(scaled, writes, (0, 0))
        for i in range(2):
            h = 2 * slab + i
            send[slab, 128 + i : 129 + i, :] = jnp.broadcast_to(last[h : h + 1, :], (1, 128))
            send[slab, 130 + i : 131 + i, :] = jnp.broadcast_to(last_slope[h : h + 1, :], (1, 128))
        send[slab, 132:136, :] = jnp.zeros((4, 128), F32)
    turned[0] = cum
    turned[1] = cum_slope
    turned[2] = step
    turned[3] = slope
    cum_out[0] = cum.T
    cum_out[1] = cum_slope.T
    rates[...] = jnp.broadcast_to(rate, (HEADS, 128))


def tangent_body(x, b, turned, rates, send):
    writes = b[...]
    cum, cum_slope, step, slope = (turned[i] for i in range(4))
    rate = rates[:, 0:1]
    spread = cum[:, TOKENS - 1 : TOKENS] - cum
    spread_slope = rate * (cum_slope - cum_slope[:, TOKENS - 1 : TOKENS])
    kept = jnp.exp(spread)
    tangents = (
        (spread * kept * step).T,
        (kept * slope + spread_slope * kept * step).T,
    )
    for slab in range(SLABS):
        values = x[:, units(slab)].astype(F32)
        for i in range(2):
            scaled = values * of_pair(tangents[i], slab)
            send[slab, 128 * i : 128 * i + 128, :] = dot_left(scaled, writes, (0, 0))


def of_rows(pair):
    return jnp.concatenate(
        [jnp.broadcast_to(pair[0:1, :], (64, 128)), jnp.broadcast_to(pair[1:2, :], (64, 128))], axis=0
    )


def kept_rows(pair):
    return of_rows(jnp.exp(pair[0:2, :]))


def group_body(got, decays, total):
    state = got[0, 0:128, :]
    whole = got[0, 128:136, :]
    decays[0] = whole
    for k in range(1, MEMBERS):
        pair = got[k, 128:136, :]
        decays[k] = pair
        state = kept_rows(pair) * state + got[k, 0:128, :]
        whole = whole + pair
    total[0:128, :] = state
    total[128:136, :] = whole


def from_groups(three, two, one):
    state = three[0:128, :]
    for group in (two, one):
        state = kept_rows(group[128:136, :]) * state + group[0:128, :]
    return state


def later_group_body(decays, got, total):
    state = got[MEMBERS - 1]
    whole = decays[MEMBERS - 1]
    for k in reversed(range(MEMBERS - 1)):
        pair = decays[k]
        state = kept_rows(pair) * state + got[k]
        whole = whole + pair
    total[0:128, :] = state
    total[128:136, :] = whole


def earlier_body(got, three, two, one, back):
    state = from_groups(three, two, one)
    for k in range(MEMBERS):
        back[k] = state
        if k < MEMBERS - 1:
            state = kept_rows(got[k, 128:136, :]) * state + got[k, 0:128, :]


def tangent_scan_body(decays, states, tangents, scanned, total):
    rate = jnp.zeros((128, 128), F32)
    bias = jnp.zeros((128, 128), F32)
    for k in range(MEMBERS):
        scanned[k, 0:128, :] = rate
        scanned[k, 128:256, :] = bias
        pair = decays[k]
        keep = kept_rows(pair)
        kept = keep * states[k]
        rate = keep * rate + tangents[k, 0:128, :] + of_rows(pair) * kept
        bias = keep * bias + tangents[k, 128:256, :] + of_rows(pair[2:4, :]) * kept
    total[0:128, :] = rate
    total[128:256, :] = bias


def causal():
    return iota((TOKENS, TOKENS), 0) >= iota((TOKENS, TOKENS), 1)


def inside_body(x, b, c, cum, turned, heads, out):
    scores = dot(c[...], b[...], (1, 1))
    mask = causal()
    left = first_head(TOKENS)
    for slab in range(SLABS):
        values = x[:, units(slab)]
        parts = []
        for h in (2 * slab, 2 * slab + 1):
            spread = cum[0, :, h : h + 1] - turned[0, h : h + 1, :]
            weights = jnp.exp(jnp.where(mask, spread, NEVER)) * turned[2, h : h + 1, :]
            parts.append(dot_left(scores * weights, values, (1, 0)))
        skip = of_pair(heads[2:3, :], slab)
        out[:, units(slab)] = jnp.where(left, parts[0], parts[1]) + skip * values.astype(F32)


def mixed_body(inside, state, c, cum, gates, cotangent, gain, carried, sums):
    reads = c[...]
    carry = jnp.exp(cum[0])
    squares = jnp.zeros((TOKENS, 128), F32)
    products = jnp.zeros((TOKENS, 128), F32)
    for slab in range(SLABS):
        part = dot_right(reads, state[units(slab), :], (1, 1)) * of_pair(carry, slab)
        carried[:, units(slab)] = part
        gated = (inside[:, units(slab)] + part) * silu(gates[:, units(slab)].astype(F32))
        squares = squares + gated * gated
        products = products + cotangent[:, units(slab)].astype(F32) * gain[:, units(slab)] * gated
    ones = jnp.ones((8, 128), F32)
    squares = dot(ones, squares, (1, 1), HIGHEST)
    products = dot(ones, products, (1, 1), HIGHEST)
    both = jnp.concatenate(
        [
            squares[0:1, 0:128],
            squares[0:1, 128:256],
            products[0:1, 0:128],
            products[0:1, 128:256],
            jnp.zeros((4, 128), F32),
        ],
        axis=0,
    )
    for k in range(8):
        sums[k] = both


def spread_sum(flat, first):
    row = iota((64, 128), 0) % 8
    return jnp.concatenate(
        [dot(flat, (row == first + i).astype(F32), (0, 0), HIGHEST) for i in range(2)], axis=0
    )


def slope_body(c, cum, gates, cotangent, gain, inside, carried, sums, seq_out, slopes, send, gains):
    flat = sums[...].reshape(64, 128)
    squares = spread_sum(flat, 0)
    products = spread_sum(flat, 2)
    inverse = lax.rsqrt(squares / INNER + EPSILON)
    pull = inverse * inverse * inverse * products / INNER
    carry = jnp.exp(cum[0])
    reads = c[...]
    for slab in range(SLABS):
        act = silu(gates[:, units(slab)].astype(F32))
        gated = (inside[:, units(slab)] + carried[:, units(slab)]) * act
        normed = gated * inverse
        weight = gain[:, units(slab)]
        cot = cotangent[:, units(slab)].astype(F32)
        seq_out[:, units(slab)] = (normed * weight).astype(BF16)
        gain_slope = jnp.sum(cot * normed, axis=0, keepdims=True)
        mixed_slope = (cot * weight * inverse - gated * pull) * act
        slopes[:, units(slab)] = mixed_slope
        send[slab] = dot_left(mixed_slope * of_pair(carry, slab), reads, (0, 0))
        gains[slab : slab + 1, :] = gain_slope


def back_body(x, b, c, cum, turned, slopes, carried, out):
    scores = dot(c[...], b[...], (1, 1))
    mask = causal()
    left = first_head(TOKENS)
    carried_sum = jnp.zeros((HEADS, TOKENS), F32)
    skip_sum = jnp.zeros((HEADS, TOKENS), F32)
    for slab in range(SLABS):
        values = x[:, units(slab)]
        slope = slopes[:, units(slab)]
        member = head_mask(slab)
        carried_sum = carried_sum + dot_right(member, slope * carried[:, units(slab)], (1, 1))
        skip_sum = skip_sum + dot_right(member, slope * values.astype(F32), (1, 1))
        top, rest = halves(slope)
        for i in range(2):
            h = 2 * slab + i
            own = left if i == 0 else jnp.logical_not(left)
            value_h = jnp.where(own, values.astype(F32), 0.0).astype(BF16)
            product = dot(top, value_h, (1, 1)) + dot(rest, value_h, (1, 1))
            spread = cum[0, :, h : h + 1] - turned[0, h : h + 1, :]
            weights = jnp.exp(jnp.where(mask, spread, NEVER)) * turned[2, h : h + 1, :]
            each = product * scores * weights
            spread_slope = cum[1, :, h : h + 1] - turned[1, h : h + 1, :]
            out[0, h : h + 1, :] = jnp.sum(each, axis=0, keepdims=True)
            out[1, h : h + 1, :] = jnp.sum(each * spread, axis=0, keepdims=True)
            out[2, h : h + 1, :] = jnp.sum(each * spread_slope, axis=0, keepdims=True)
    out[3] = carried_sum
    out[4] = skip_sum


def meet_body(got, scanned, out):
    for i in range(2):
        met = got[0] * scanned[0, 128 * i : 128 * i + 128, :]
        for k in range(1, MEMBERS):
            met = met + got[k] * scanned[k, 128 * i : 128 * i + 128, :]
        out[128 * i : 128 * i + 128, :] = met


def heads_body(place, met, tangents, three, two, one, turned, inner, heads, gains, send):
    later = from_groups(three, two, one)
    rate_sum = met[0:128, :] + later * tangents[0:128, :]
    bias_sum = met[128:256, :] + later * tangents[128:256, :]

    def total(a):
        return jnp.sum(a, axis=1, keepdims=True)

    cum, cum_slope, step, slope = (turned[i] for i in range(4))
    carried = inner[3]
    rate_slope = total(inner[1] + carried * cum)
    bias_slope = total(inner[0] * slope / step) - jnp.exp(column(heads, 0)) * total(
        inner[2] + carried * cum_slope
    )
    skip_slope = total(inner[4])
    row = iota((HEADS, 1), 0)
    for i in range(2):
        own = row == 2 * place[0] + i
        half = slice(64 * i, 64 * i + 64)
        rate_slope = rate_slope + jnp.where(own, total(jnp.sum(rate_sum[half], axis=0, keepdims=True)), 0.0)
        bias_slope = bias_slope + jnp.where(own, total(jnp.sum(bias_sum[half], axis=0, keepdims=True)), 0.0)
    lane = iota((HEADS, 8), 1)
    table = jnp.where(
        lane == 0, rate_slope, jnp.where(lane == 1, bias_slope, jnp.where(lane == 2, skip_slope, 0.0))
    )
    unit = (iota((HEADS, 128), 0) == iota((HEADS, 128), 1)).astype(F32)
    rows = dot(table, unit, (0, 0), HIGHEST)
    for k in range(4):
        for i in range(3):
            send[k, :, 128 * i : 128 * i + 128] = rows[i : i + 1, :]
        for slab in range(SLABS):
            send[k, :, 384 + 128 * slab : 512 + 128 * slab] = gains[slab : slab + 1, :]


def near_body(got, send):
    row = got[0] + got[1] + got[2] + got[3]
    for k in range(16):
        send[k] = row


def before_body(state, reads, writes, out):
    for r in range(2):
        out[r, 0:4, :] = dot(reads[r], state[r], (1, 1))
        meet = dot(writes[r], reads[r], (1, 1))
        out[r, 4:8, 0:128] = jnp.concatenate([meet, jnp.zeros((4, 124), F32)], axis=1)


def decode_body(
    lengths, got, heads, slow, raw, values, gates, before, gated_out, sums, weights_out, gains,
    head_sum, blended,
):
    total = got[0]
    for k in range(1, 16):
        total = total + got[k]
    for slab in range(SLABS):
        gains[slab : slab + 1, :] = total[:, 384 + 128 * slab : 512 + 128 * slab]
    total = jnp.concatenate([total[:, 128 * i : 128 * i + HEADS] for i in range(3)], axis=0)
    head_sum[...] = total
    blend = KEEP_SHARE * slow[...] + (1.0 - KEEP_SHARE) * (heads[...] - STEP_RATE * total)
    blended[...] = blend
    step = softplus(raw[...] + blend[1:2, :])
    log_decay = -jnp.exp(blend[0:1, :]) * step
    spread = (iota((HEADS, UNITS), 0) == iota((HEADS, UNITS), 1) // HEAD_DIM).astype(F32)
    table = jnp.concatenate([step, log_decay, jnp.broadcast_to(blend[2:3, :], (8, HEADS))], axis=0)
    wide = dot(table, spread, (1, 0), HIGHEST)
    skip = wide[16:17, :]
    row8 = iota((8, 128), 0)
    totals = jnp.zeros((8, 128), F32)
    for r in range(2):
        length = lengths[r]
        cum = []
        drive = []
        rows = values[r].astype(F32)
        for k in range(STEPS):
            at = 4 * r + k
            log_k = wide[8 + at : 9 + at, :]
            cum.append(log_k if k == 0 else cum[-1] + log_k)
            drive.append(wide[at : at + 1, :] * rows[k : k + 1, :])
        act = silu(gates[r].astype(F32))
        for k in range(STEPS):
            read = jnp.exp(cum[k]) * before[r, k : k + 1, :] + skip * rows[k : k + 1, :]
            for j in range(k + 1):
                kept = drive[j] if j == k else jnp.exp(cum[k] - cum[j]) * drive[j]
                read = read + kept * before[r, 4 + j : 5 + j, k : k + 1]
            gated = read * act[k : k + 1, :]
            gated_out[r, k : k + 1, :] = gated
            squares = jnp.sum(gated * gated, axis=1, keepdims=True)
            totals = jnp.where(row8 == 4 * r + k, squares, totals)
        end = cum[0]
        for k in range(1, STEPS):
            end = jnp.where(length > k, cum[k], end)
        weights = [jnp.exp(end)]
        for j in range(STEPS):
            live = length > j
            weights.append(jnp.where(live, jnp.exp(jnp.where(live, end - cum[j], 0.0)) * drive[j], 0.0))
        weights.append(jnp.zeros((3, UNITS), F32))
        weights_out[r] = jnp.concatenate(weights, axis=0)
    for k in range(8):
        sums[k] = totals


def final_body(weights, writes, state, final):
    first = (iota((8, STATE), 0) == 0).astype(F32)
    for r in range(2):
        wide_writes = jnp.concatenate(
            [jnp.zeros((1, STATE), F32), writes[r].astype(F32), jnp.zeros((3, STATE), F32)], axis=0
        )
        kept = dot(weights[r], first, (0, 0), HIGHEST)
        fresh = dot(weights[r], wide_writes, (0, 0), HIGHEST)
        final[r] = kept * state[r].astype(F32) + fresh


def rows_body(lengths, got, gated, gain, gain_slope, slow, out, gain_out):
    blend = KEEP_SHARE * slow[...] + (1.0 - KEEP_SHARE) * (gain[...] - STEP_RATE * gain_slope[...])
    gain_out[...] = blend
    total = got[0]
    for k in range(1, 8):
        total = total + got[k]
    inverse = lax.rsqrt(total / INNER + EPSILON)
    for slab in range(SLABS):
        for r in range(2):
            shown = gated[r, :, units(slab)] * inverse[4 * r : 4 * r + 4, :] * blend[slab : slab + 1, :]
            live = iota((STEPS, 128), 0) < lengths[r]
            out[r, :, units(slab)] = jnp.where(live, shown, 0.0).astype(BF16)


def exchange(value, axes):
    return lax.all_to_all(value, axes, split_axis=0, concat_axis=0, tiled=True)


def shifted(value, by):
    pairs = [(k, k + by) for k in range(FAR) if 0 <= k + by < FAR]
    return lax.ppermute(value, "far", pairs)


def on_device(
    train_values,
    train_gates,
    train_writes,
    train_reads,
    train_steps,
    out_cotangent,
    head_params,
    norm_gain,
    slow_heads,
    slow_gain,
    roll_state,
    roll_values,
    roll_gates,
    roll_writes,
    roll_reads,
    roll_steps,
    roll_lengths,
):
    x, gates, cotangent = train_values[0], train_gates[0], out_cotangent[0]
    b, c, raw = train_writes[0], train_reads[0], train_steps[0].T
    gain = norm_gain.reshape(1, UNITS)
    wide = (TOKENS, UNITS)
    group = (136, STATE)
    tile = (8, 8, 128)

    bound = lax.optimization_barrier
    send, cum, turned, rates = call(
        state_body,
        [
            ((MEMBERS, 136, STATE), F32),
            ((2, TOKENS, HEADS), F32),
            ((4, HEADS, TOKENS), F32),
            ((HEADS, 128), F32),
        ],
        x, b, raw, head_params,
        hbm=(0, 1, 2, 3),
        vmem=60 * 2**20,
        scratch=(
            pltpu.VMEM((TOKENS, UNITS), BF16),
            pltpu.VMEM((TOKENS, STATE), BF16),
            pltpu.VMEM((HEADS, TOKENS), F32),
            pltpu.VMEM((3, HEADS), F32),
            pltpu.SemaphoreType.DMA((4,)),
        ),
    )
    got = exchange(send, GROUP)
    (send,) = call(tangent_body, [((MEMBERS, 256, STATE), F32)], x, b, turned, rates)
    (inside,) = call(
        inside_body, [(wide, F32)], x, b, c, cum, turned, head_params
    )
    decays, total = call(group_body, [(tile, F32), (group, F32)], got)
    send, total = bound((send, total))
    tangents = exchange(send, GROUP)
    groups = [shifted(total, by) for by in (3, 2, 1)]
    (back,) = call(
        earlier_body, [((MEMBERS, 128, STATE), F32)], got, *groups, after=(tangents,)
    )
    state_in = exchange(back, GROUP).reshape(UNITS, STATE)
    scanned, group_tangents = call(
        tangent_scan_body,
        [((MEMBERS, 256, STATE), F32), ((256, STATE), F32)],
        decays, back, tangents,
    )
    carried, sums = call(
        mixed_body, [(wide, F32), (tile, F32)], inside, state_in, c, cum, gates, cotangent, gain
    )
    sums = exchange(sums, "shd")
    seq_out, slopes, send, gains = call(
        slope_body,
        [(wide, BF16), (wide, F32), ((MEMBERS, 128, STATE), F32), ((8, 128), F32)],
        c, cum, gates, cotangent, gain, inside, carried, sums,
    )
    upward = exchange(send, GROUP)
    (total,) = call(later_group_body, [(group, F32)], decays, upward)
    groups = [shifted(total, -by) for by in (3, 2, 1)]
    (met,) = call(meet_body, [((256, STATE), F32)], upward, scanned)
    (inner,) = call(
        back_body, [((5, HEADS, TOKENS), F32)], x, b, c, cum, turned, slopes, carried
    )
    flat_state = roll_state.reshape(2, UNITS, STATE)
    (before,) = call(before_body, [((2, 8, UNITS), F32)], flat_state, roll_reads, roll_writes)
    place = (2 * lax.axis_index("near") + lax.axis_index("ctx_1")).reshape(1)
    (send,) = call(
        heads_body,
        [((4, 1, 1408), F32)],
        place, met, group_tangents, *groups, turned, inner, head_params, gains,
        smem=(0,),
    )
    near = exchange(send, ("grp", "ctx_1"))
    (send,) = call(near_body, [((16, 1, 1408), F32)], near)
    far = exchange(send, ("far", "near"))
    gated, sums, weights, gain_slope, head_sum, blend_heads = call(
        decode_body,
        [
            ((2, STEPS, UNITS), F32),
            (tile, F32),
            ((2, 8, UNITS), F32),
            ((8, 128), F32),
            ((3, HEADS), F32),
            ((3, HEADS), F32),
        ],
        roll_lengths, far, head_params, slow_heads, roll_steps.reshape(8, HEADS), roll_values,
        roll_gates, before,
        smem=(0,),
    )
    sums = exchange(sums, "shd")
    (final,) = call(
        final_body, [((2, UNITS, STATE), F32)], weights, roll_writes, flat_state
    )
    roll_out, blend_gain = call(
        rows_body,
        [((2, STEPS, UNITS), BF16), ((8, 128), F32)],
        roll_lengths, sums, gated, norm_gain.reshape(8, 128), gain_slope, slow_gain.reshape(8, 128),
        smem=(0,),
    )
    return (
        seq_out[None],
        head_sum,
        gain_slope.reshape(UNITS),
        blend_heads,
        blend_gain.reshape(UNITS),
        roll_out,
        final.reshape(2, HEADS, HEAD_DIM, STATE),
    )


def solution(mesh):
    split = Mesh(
        mesh.devices.reshape(mesh.shape["grp"], FAR, 4, 2, mesh.shape["shd"]),
        ("grp", "far", "near", "ctx_1", "shd"),
    )
    return jax.shard_map(
        on_device,
        mesh=split,
        in_specs=(
            P("grp", CTX, "shd"),
            P("grp", CTX, "shd"),
            P("grp", CTX, "shd"),
            P("grp", CTX, "shd"),
            P("grp", CTX, "shd"),
            P("grp", CTX, "shd"),
            P(None, "shd"),
            P("shd"),
            P(None, "shd"),
            P("shd"),
            P(GRP_CTX, "shd", None, None),
            P(GRP_CTX, None, "shd"),
            P(GRP_CTX, None, "shd"),
            P(GRP_CTX, None, "shd"),
            P(GRP_CTX, None, "shd"),
            P(GRP_CTX, None, "shd"),
            P(GRP_CTX),
        ),
        out_specs=(
            P("grp", CTX, "shd"),
            P(None, "shd"),
            P("shd"),
            P(None, "shd"),
            P("shd"),
            P(GRP_CTX, None, "shd"),
            P(GRP_CTX, "shd", None, None),
        ),
        check_vma=False,
    )
```
